256 devices in a mesh: wide: 16 (over y, x_hi, core), narrow: 16 (over z, x_lo).
Axes of the slice: x: 4 (x_hi: 2, x_lo: 2; x = x_hi * 2 + x_lo), y: 4, z: 8, core: 2. Of those that a mesh axis runs over, the one named last changes fastest.
Arguments:
- sequence_activity: bfloat16 [32, 4096, 256], P('narrow', 'wide'), may hold values from -6 to 6
- couple_activity: bfloat16 [512, 4096, 128], P('wide', 'narrow'), may hold values from -6 to 6
- sequence_valid_flags: int32 [32], replicated, may hold values 0 or 1
- position_valid_flags: int32 [4096], P('wide'), may hold values 0 or 1
- attend_scale_vector: float32 [256], replicated, may hold values from 0.1 to 1.9
- asking_matrix: bfloat16 [256, 256], replicated, may hold values from -10 to 10
- lookup_matrix: bfloat16 [256, 256], replicated, may hold values from -0.375 to 0.375
- content_matrix: bfloat16 [256, 256], replicated, may hold values from -0.375 to 0.375
- sigmoid_matrix: bfloat16 [256, 256], replicated, may hold values from -0.375 to 0.375
- attend_final_matrix: bfloat16 [256, 256], replicated, may hold values from -0.375 to 0.375
- couple_scale_vector: float32 [128], replicated, may hold values from 0.1 to 1.9
- headwise_additive_matrix: bfloat16 [128, 8], replicated, may hold values from -4 to 4
- product_scale_vector: float32 [256], replicated, may hold values from 0.1 to 1.9
- first_factor_matrix: bfloat16 [256, 32], replicated, may hold values from -0.375 to 0.375
- other_factor_matrix: bfloat16 [256, 32], replicated, may hold values from -0.375 to 0.375
- product_mapping_matrix: bfloat16 [1024, 128], replicated, may hold values from -0.1875 to 0.1875
Outputs:
- fresh_target_sequences: bfloat16 [32, 512, 256], P('narrow', 'wide')
- pair_strip_output: bfloat16 [512, 4096, 128], P('wide', 'narrow')
The draws below stay inside these ranges and needn't reach their ends.
All inputs are finite; a program needn't handle non-finite values. No bound on the sum of `position_valid_flags` on one device may be relied on, other than what follows from the above.
Results may differ from the reference program's by a relative error of at most 0.012.
The reference program's roundings to bfloat16 on the way count: a program that leaves them out, or rounds other values in their place, can miss the bound.
Values may be sent and summed in bfloat16 or wider, within the bound.
No kernel may reach another device: no remote copies, remote signals or barrier semaphores. Data moves between devices by JAX's collectives and lax.ppermute only.
A program may use at most 128 MiB of HBM per device.

```python
import jax
import jax.numpy as jnp
from jax import lax

SEQUENCE_FEATURES = 256
CZ = 128
HEADS = 8
HEAD = 32
PRODUCT_FACTORS = 32
TARGET_STRIDE = 8
CHAIN_POSITIONS = 4096
SEQUENCE_DEPTH = 32
BAND = 512


def draw_asking_matrix(key, part):
    key = jax.random.fold_in(key, 11)
    starting_position = jax.random.truncated_normal(jax.random.fold_in(key, 1), -4.0, 4.0, (SEQUENCE_FEATURES, SEQUENCE_FEATURES), jnp.float32) * SEQUENCE_FEATURES ** (-0.5)
    return starting_position.astype(jnp.bfloat16)


def place_ends(values, key, smallest, largest):
    dims = values.shape
    spot = [jax.random.randint(jax.random.fold_in(key, axis), (), 0, dims[axis]) for axis in range(len(dims))]
    values = values.at[tuple(spot)].set(smallest)
    longest = dims.index(max(dims))
    spot[longest] = (spot[longest] + 1) % dims[longest]
    return values.at[tuple(spot)].set(largest)


def steps_of(rng, extent, cuts, smallest, top_value):
    loudness = 1.0
    for dim, shards_of in cuts:
        steps = jax.random.uniform(jax.random.fold_in(jax.random.fold_in(rng, 6), dim), (shards_of,), jnp.float32, smallest / len(cuts), top_value / len(cuts))
        loudness = loudness * jnp.repeat(jnp.exp(steps), extent[dim] // shards_of).reshape((-1,) + (1,) * (len(extent) - 1 - dim))
    return loudness


def scatter_about(stream_key, extent, scale, reach, shards=(), dtype=jnp.bfloat16):
    level = steps_of(stream_key, extent, shards, -0.22, 0.18) if shards else 1.0
    result = jax.random.normal(stream_key, extent, jnp.float32) * scale * level
    return jnp.minimum(jnp.maximum(result, -reach), reach).astype(dtype)


def setup_inputs(seed: int = 0) -> dict:
    streams_of = jax.random.split(jax.random.key(seed), 17)
    sequence_activity = scatter_about(streams_of[0], (SEQUENCE_DEPTH, CHAIN_POSITIONS, SEQUENCE_FEATURES), 1.0, 6.0, ((0, 16), (1, 16)))
    couple_activity = scatter_about(streams_of[1], (BAND, CHAIN_POSITIONS, CZ), 1.0, 6.0, ((0, 16), (1, 16)))
    sequence_valid_flags = place_ends((jax.random.randint(streams_of[2], (SEQUENCE_DEPTH,), 0, 4) < 3).astype(jnp.int32), jax.random.fold_in(streams_of[2], 1), 0, 1)
    position_valid_flags = place_ends((jax.random.randint(streams_of[3], (CHAIN_POSITIONS,), 0, 16) < 15).astype(jnp.int32), jax.random.fold_in(streams_of[3], 1), 0, 1)
    attend_scale_vector = jnp.clip(1.0 + 0.18 * jax.random.normal(streams_of[4], (SEQUENCE_FEATURES,), jnp.float32), 0.1, 1.9)
    asking_matrix = draw_asking_matrix(jax.random.fold_in(streams_of[16], 71), 0)
    lookup_matrix = scatter_about(streams_of[6], (SEQUENCE_FEATURES, SEQUENCE_FEATURES), SEQUENCE_FEATURES ** -0.5, 0.375)
    content_matrix = scatter_about(streams_of[7], (SEQUENCE_FEATURES, SEQUENCE_FEATURES), SEQUENCE_FEATURES ** -0.5, 0.375)
    sigmoid_matrix = scatter_about(streams_of[8], (SEQUENCE_FEATURES, SEQUENCE_FEATURES), SEQUENCE_FEATURES ** -0.5, 0.375)
    attend_final_matrix = scatter_about(streams_of[9], (SEQUENCE_FEATURES, SEQUENCE_FEATURES), SEQUENCE_FEATURES ** -0.5, 0.375)
    couple_scale_vector = jnp.clip(1.0 + 0.18 * jax.random.normal(streams_of[10], (CZ,), jnp.float32), 0.1, 1.9)
    headwise_additive_matrix = scatter_about(streams_of[11], (CZ, HEADS), (3.0 * CZ ** -0.5), 4.0)
    product_scale_vector = jnp.clip(1.0 + 0.18 * jax.random.normal(streams_of[12], (SEQUENCE_FEATURES,), jnp.float32), 0.1, 1.9)
    first_factor_matrix = scatter_about(streams_of[13], (SEQUENCE_FEATURES, PRODUCT_FACTORS), SEQUENCE_FEATURES ** -0.5, 0.375)
    other_factor_matrix = scatter_about(streams_of[14], (SEQUENCE_FEATURES, PRODUCT_FACTORS), SEQUENCE_FEATURES ** -0.5, 0.375)
    product_mapping_matrix = scatter_about(streams_of[15], (PRODUCT_FACTORS * PRODUCT_FACTORS, CZ), (PRODUCT_FACTORS * PRODUCT_FACTORS) ** -0.5, 0.1875)
    return {"sequence_activity": sequence_activity, "couple_activity": couple_activity, "sequence_valid_flags": sequence_valid_flags, "position_valid_flags": position_valid_flags, "attend_scale_vector": attend_scale_vector, "asking_matrix": asking_matrix, "lookup_matrix": lookup_matrix, "content_matrix": content_matrix, "sigmoid_matrix": sigmoid_matrix, "attend_final_matrix": attend_final_matrix, "couple_scale_vector": couple_scale_vector, "headwise_additive_matrix": headwise_additive_matrix, "product_scale_vector": product_scale_vector, "first_factor_matrix": first_factor_matrix, "other_factor_matrix": other_factor_matrix, "product_mapping_matrix": product_mapping_matrix}


def standardize_features(values, gain):
    values = values.astype(jnp.float32)
    center = values - lax.optimization_barrier(jnp.mean(values, axis=-1, keepdims=True))
    spread = lax.optimization_barrier(jnp.mean(center * center, axis=-1, keepdims=True))
    return center * lax.rsqrt(spread + 1e-05) * gain

def reference(sequence_activity, couple_activity, sequence_valid_flags, position_valid_flags, attend_scale_vector, asking_matrix, lookup_matrix, content_matrix, sigmoid_matrix, attend_final_matrix, couple_scale_vector, headwise_additive_matrix, product_scale_vector, first_factor_matrix, other_factor_matrix, product_mapping_matrix):
    sequence_total, band_extent, feature_width = sequence_activity.shape
    couple_band_slice = band_extent // TARGET_STRIDE
    standardized_sequences = standardize_features(sequence_activity, attend_scale_vector).astype(jnp.bfloat16)
    band_in = standardized_sequences.reshape(sequence_total, couple_band_slice, TARGET_STRIDE, feature_width)[:, :, 0]
    query = (jnp.dot(band_in, asking_matrix, preferred_element_type=jnp.float32) * HEAD ** (-0.5)).astype(jnp.bfloat16)
    query = query.reshape(sequence_total, couple_band_slice, HEADS, HEAD)
    keys = jnp.dot(standardized_sequences, lookup_matrix, preferred_element_type=jnp.float32).astype(jnp.bfloat16).reshape(sequence_total, band_extent, HEADS, HEAD)
    values = jnp.dot(standardized_sequences, content_matrix, preferred_element_type=jnp.float32).astype(jnp.bfloat16).reshape(sequence_total, band_extent, HEADS, HEAD)
    gate = jax.nn.sigmoid(jnp.dot(band_in, sigmoid_matrix, preferred_element_type=jnp.float32))
    pair_normed = standardize_features(couple_activity, couple_scale_vector).astype(jnp.bfloat16)
    bias = jnp.einsum('rjc,ch->hrj', pair_normed.astype(jnp.float32), headwise_additive_matrix.astype(jnp.float32)).astype(jnp.bfloat16)
    extra = bias.astype(jnp.float32) + 1000000000.0 * (position_valid_flags.astype(jnp.float32) - 1.0)[None, None, :]

    def attend_row(items):
        q_row, k_row, v_row = items
        scores = jnp.einsum('rhd,jhd->hrj', q_row.astype(jnp.float32), k_row.astype(jnp.float32)) + extra
        top = lax.optimization_barrier(jnp.max(scores, axis=-1, keepdims=True))
        expo = jnp.exp(scores - top)
        total = lax.optimization_barrier(jnp.sum(expo, axis=-1))
        mixed = jnp.einsum('hrj,jhd->hrd', expo.astype(jnp.bfloat16).astype(jnp.float32), v_row.astype(jnp.float32))
        return mixed / total[..., None]
    attended = lax.map(attend_row, (query, keys, values))
    attended = attended.transpose(0, 2, 1, 3).reshape(sequence_total, couple_band_slice, feature_width)
    gate_applied = (gate * attended).astype(jnp.bfloat16)
    prior_band_slice = sequence_activity.reshape(sequence_total, couple_band_slice, TARGET_STRIDE, feature_width)[:, :, 0]
    fresh_target_sequences = (prior_band_slice.astype(jnp.float32) + jnp.dot(gate_applied, attend_final_matrix, preferred_element_type=jnp.float32)).astype(jnp.bfloat16)
    refreshed_sequences = sequence_activity.reshape(sequence_total, couple_band_slice, TARGET_STRIDE, feature_width).at[:, :, 0].set(fresh_target_sequences).reshape(sequence_total, band_extent, feature_width)
    normalized_second2 = standardize_features(refreshed_sequences, product_scale_vector).astype(jnp.bfloat16)
    live = sequence_valid_flags.astype(jnp.float32)[:, None] * position_valid_flags.astype(jnp.float32)[None, :]
    left = (jnp.dot(normalized_second2, first_factor_matrix, preferred_element_type=jnp.float32) * live[..., None]).astype(jnp.bfloat16)
    right = (jnp.dot(normalized_second2, other_factor_matrix, preferred_element_type=jnp.float32) * live[..., None]).astype(jnp.bfloat16)
    left_band = left.reshape(sequence_total, couple_band_slice, TARGET_STRIDE, left.shape[-1])[:, :, 0]
    nvalid = jnp.sum(sequence_valid_flags.astype(jnp.float32))
    divisor = jnp.maximum(nvalid * position_valid_flags.reshape(couple_band_slice, TARGET_STRIDE)[:, 0].astype(jnp.float32), 1.0)
    blocks = couple_band_slice // 8
    left_blocks = left_band.reshape(sequence_total, blocks, 8, left.shape[-1]).transpose(1, 0, 2, 3)
    pair_blocks = couple_activity.reshape(blocks, 8, band_extent, couple_activity.shape[-1])
    divisor_blocks = divisor.reshape(blocks, 8)
    right_f = right.astype(jnp.float32)

    def outer_block(items):
        left_piece, pair_piece, divisor_piece = items
        outer = jnp.einsum('sic,sjd->ijcd', left_piece.astype(jnp.float32), right_f).astype(jnp.bfloat16)
        outer = outer.reshape(8 * band_extent, -1)
        projected = jnp.dot(outer, product_mapping_matrix, preferred_element_type=jnp.float32).reshape(8, band_extent, -1)
        return (pair_piece.astype(jnp.float32) + projected / divisor_piece[:, None, None]).astype(jnp.bfloat16)
    pair_strip_output = lax.map(outer_block, (left_blocks, pair_blocks, divisor_blocks)).reshape(couple_band_slice, band_extent, couple_activity.shape[-1])
    return (fresh_target_sequences, pair_strip_output)
```

```python
import jax
import jax.numpy as jnp
from jax import lax
from jax.experimental import pallas as pl
from jax.experimental.pallas import tpu as pltpu
from jax.sharding import Mesh, PartitionSpec as P

EPS = 1e-05
BIG = 1000000000.0
F32 = jnp.float32
BF16 = jnp.bfloat16
VMEM = 48 * 1024 * 1024
ALL = ("q", "c", "z", "x")


def dot(a, b, dims):
    return lax.dot_general(a, b, (dims, ((), ())), preferred_element_type=F32)


NN = ((1,), (0,))
NT = ((1,), (1,))
TN = ((0,), (0,))
TT = ((0,), (1,))


def center_and_scale(values):
    center = values - jnp.mean(values, axis=-1, keepdims=True)
    spread = jnp.mean(center * center, axis=-1, keepdims=True)
    return center * lax.rsqrt(spread + EPS)


def front_kernel(
    pair_ref,
    seq_ref,
    live_ref,
    flags_ref,
    g1_ref,
    ask_ref,
    look_ref,
    cont_ref,
    sig_ref,
    gp_ref,
    head_ref,
    g2_ref,
    other_ref,
    msg_ref,
    gate_ref,
    right_ref,
    bias_scr,
    norm_scr,
):
    step = pl.program_id(0)
    rows = pair_ref.shape[0]

    pair = pair_ref[...].reshape(rows * 256, 128).astype(F32)
    pair = (center_and_scale(pair) * gp_ref[...]).astype(BF16)
    bias = dot(head_ref[...], pair, TT)
    for r in range(rows):
        for i in range(2):
            bias_scr[i, pl.ds(pl.multiple_of((step * rows + r) * 8, 8), 8), :] = bias[
                :, r * 256 + i * 128 : r * 256 + i * 128 + 128
            ]

    @pl.when(step == 0)
    def _():
        base = center_and_scale(seq_ref[...].astype(F32))
        normed = (base * g1_ref[...]).astype(BF16)
        keys = dot(look_ref[...], normed, TT).astype(BF16)
        values = dot(cont_ref[...], normed, TT).astype(BF16)
        for h in range(8):
            for s in range(2):
                cut = (slice(h * 32, h * 32 + 32), slice(s * 256, s * 256 + 256))
                msg_ref[h, 32 + s * 32 : 64 + s * 32, :] = keys[cut]
                msg_ref[h, 96 + s * 32 : 128 + s * 32, :] = values[cut]
        wide = normed.astype(F32)
        for i in range(2):
            norm_scr[i] = wide[:, i * 128 : (i + 1) * 128]
        band = jnp.concatenate(
            [norm_scr[i, pl.ds(0, 64, stride=8), :] for i in range(2)], axis=1
        ).astype(BF16)
        gate_ref[...] = jax.nn.sigmoid(dot(band, sig_ref[...], NN))
        query = (dot(band, ask_ref[...], NN) * 32 ** (-0.5)).astype(BF16).astype(F32)
        flags = flags_ref[...].astype(F32)
        row = lax.broadcasted_iota(jnp.int32, (16, 128), 0)
        mask = jnp.where(row == 0, flags[0:1], jnp.where(row == 1, flags[1:2], 0.0))
        for h in range(8):
            parts = [
                query[s * 32 + g * 16 : s * 32 + g * 16 + 16, h * 32 : h * 32 + 32]
                for g in range(2)
                for s in range(2)
            ]
            msg_ref[h, 160:176, :] = jnp.concatenate(parts + [mask], axis=1).astype(BF16)
        again = (base * g2_ref[...]).astype(BF16)
        right = dot(other_ref[...], again, TT)
        for s in range(2):
            right_ref[s] = (right[:, s * 256 : (s + 1) * 256] * live_ref[s : s + 1, :]).astype(BF16)

    @pl.when(step == pl.num_programs(0) - 1)
    def _():
        for h in range(8):
            for i in range(2):
                msg_ref[h, 0:32, i * 128 : i * 128 + 128] = bias_scr[
                    i, pl.ds(h, 32, stride=8), :
                ].astype(BF16)


def split3(value):
    high = value.astype(BF16).astype(F32)
    rest = value - high
    middle = rest.astype(BF16).astype(F32)
    return high, middle, rest - middle


def attend_kernel(
    place_ref, own_ref, swapped_ref, kva_ref, kvb_ref, bias_ref, x0_ref, x1_ref, out_ref, extra_scr
):
    c, x = place_ref[0], place_ref[1]
    lane = lax.broadcasted_iota(jnp.int32, (128, 128), 1)
    block, inner = lane // 32, lane % 32
    first_x = jnp.where(x == 0, x0_ref[...], x1_ref[...])
    second_x = jnp.where(x == 0, x1_ref[...], x0_ref[...])
    for q in range(8):
        out_ref[q, 0, 16:48, :] = first_x
        out_ref[q, 1, 16:48, :] = second_x
    mask = jnp.concatenate(
        [kva_ref[k, 128 + i : 129 + i, 128:256].astype(F32) for k in range(8) for i in range(2)], axis=1
    )
    penalty = BIG * (mask - 1.0)
    for g in range(2):
        for k in range(8):
            piece = bias_ref[k, :, g * 16 : g * 16 + 16, :].reshape(128, 256).astype(F32)
            extra_scr[g, :, k * 256 : (k + 1) * 256] = piece + penalty[:, k * 256 : (k + 1) * 256]
    own = own_ref[...].reshape(128, 128)
    swapped = swapped_ref[...].reshape(128, 128)
    for a in range(2):
        kv_ref = (kva_ref, kvb_ref)[a]
        half = c ^ a
        query = jnp.where(half == x, own, swapped).astype(F32)
        keys = jnp.concatenate([kv_ref[k, 0:64, :] for k in range(8)], axis=1)
        values = jnp.concatenate([kv_ref[k, 64:128, :] for k in range(8)], axis=1)
        keys = jnp.concatenate([keys, keys], axis=0)
        values = jnp.concatenate([values, values], axis=0)
        mixed = jnp.zeros((128, 128), F32)
        stats = jnp.zeros((128, 128), F32)
        for g in range(2):
            for s in range(2):
                here = block == g * 2 + s
                picked = jnp.where(here, query, 0.0).astype(BF16)
                scores = dot(picked, keys, NN) + extra_scr[g]
                top = jnp.max(scores, axis=1, keepdims=True)
                expo = jnp.exp(scores - top)
                total = jnp.sum(expo, axis=1, keepdims=True)
                part = dot(expo.astype(BF16), values, NT)
                mixed = jnp.where(here, part / total, mixed)
                for t, piece in enumerate(split3(top) + split3(total)):
                    stats = jnp.where(here & (inner == t), piece, stats)
        joined = jnp.concatenate([mixed, stats], axis=1).astype(BF16)
        for q in range(8):
            out_ref[q, half, 0:16, :] = joined[q * 16 : q * 16 + 16]


def refresh_kernel(
    parts_ref, gate_ref, prior_ref, final_ref, g2_ref, first_ref, other_ref, live_ref, fresh_ref, sides_ref
):
    rows = lax.broadcasted_iota(jnp.int32, (128, 128), 0)
    lanes = lax.broadcasted_iota(jnp.int32, (128, 128), 1)
    spread = [jnp.where(rows == (lanes // 32) * 32 + t, 1.0, 0.0).astype(BF16) for t in range(6)]
    tops, totals, mixes = [], [], []
    for x in range(2):
        mixes.append(
            jnp.concatenate([parts_ref[2 * h + x, 0:16, 0:128] for h in range(8)], axis=0).astype(F32)
        )
        stats = jnp.concatenate([parts_ref[2 * h + x, 0:16, 128:256] for h in range(8)], axis=0)
        wide = [dot(stats, spread[t], NN) for t in range(6)]
        tops.append(wide[0] + wide[1] + wide[2])
        totals.append(wide[3] + wide[4] + wide[5])
    top = jnp.maximum(tops[0], tops[1])
    weights = [totals[i] * jnp.exp(tops[i] - top) for i in range(2)]
    attended = (weights[0] * mixes[0] + weights[1] * mixes[1]) / (weights[0] + weights[1])
    lined = []
    for s in range(2):
        for g in range(2):
            cut = (g * 2 + s) * 32
            lined.append(
                jnp.concatenate(
                    [attended[h * 16 : h * 16 + 16, cut : cut + 32] for h in range(8)], axis=1
                )
            )
    attended = jnp.concatenate(lined, axis=0)
    gated = (gate_ref[...] * attended).astype(BF16)
    fresh = (prior_ref[...].astype(F32) + dot(gated, final_ref[...], NN)).astype(BF16)
    fresh_ref[...] = fresh
    again = (center_and_scale(fresh.astype(F32)) * g2_ref[...]).astype(BF16)
    left = dot(again, first_ref[...], NN) * live_ref[...]
    right = dot(again, other_ref[...], NN) * live_ref[...]
    sides_ref[...] = jnp.concatenate(
        [left[0:32], right[0:32], left[32:64], right[32:64]], axis=1
    ).astype(BF16)


def outer_kernel(divisor_ref, right_ref, left_ref, map_ref, pair_ref, out_ref, scr):
    step = pl.program_id(0)
    rows = pair_ref.shape[0]
    for r in range(0, rows, 2):
        mapped = dot(left_ref[r * 32 : (r + 2) * 32, :], map_ref[...], NN).astype(BF16)
        for d in range(32):
            for i in range(2):
                scr[d * 32 : d * 32 + 32, i * 128 : i * 128 + 128] = mapped[
                    i * 32 : i * 32 + 32, d * 128 : d * 128 + 128
                ]
        projected = dot(right_ref[...], scr[...], NN)
        for i in range(2):
            scale = 1.0 / divisor_ref[step * rows + r + i]
            out_ref[r + i] = (
                pair_ref[r + i].astype(F32) + projected[:, i * 128 : (i + 1) * 128] * scale
            ).astype(BF16)


def gather(value, axes, count):
    tiled = jnp.broadcast_to(value[None], (count,) + value.shape)
    return lax.all_to_all(tiled, axes, 0, 0, tiled=True)


def whole(shape):
    return pl.BlockSpec(shape, lambda *_: (0,) * len(shape))


def params():
    return pltpu.CompilerParams(vmem_limit_bytes=VMEM)


MIRROR = [(w * 16 + n, n * 16 + w) for w in range(16) for n in range(16)]
MIRROR_NEXT = [(w * 16 + n, n * 16 + (w ^ 1)) for w in range(16) for n in range(16)]
ACROSS = [(a * 2 + b, b * 2 + a) for a in range(2) for b in range(2)]
ACROSS_NEXT = [(a * 2 + b, (1 - b) * 2 + a) for a in range(2) for b in range(2)]
SWAP = [(0, 1), (1, 0)]


def local(
    sequence_activity,
    couple_activity,
    sequence_valid_flags,
    position_valid_flags,
    attend_scale_vector,
    asking_matrix,
    lookup_matrix,
    content_matrix,
    sigmoid_matrix,
    attend_final_matrix,
    couple_scale_vector,
    headwise_additive_matrix,
    product_scale_vector,
    first_factor_matrix,
    other_factor_matrix,
    product_mapping_matrix,
):
    c, z, x = lax.axis_index("c"), lax.axis_index("z"), lax.axis_index("x")
    row_live = lax.dynamic_slice_in_dim(sequence_valid_flags, (z * 2 + x) * 2, 2).astype(F32)
    positions = position_valid_flags.astype(F32)
    live = row_live[:, None] * positions[None, :]
    live_band = live.reshape(2, 32, 8)[:, :, 0].reshape(64, 1)
    prior = sequence_activity.reshape(64, 8, 256)[:, 0]
    g2 = product_scale_vector.reshape(1, 256)

    seq = sequence_activity.reshape(512, 256)
    message, gate, right = pl.pallas_call(
        front_kernel,
        grid=(4,),
        in_specs=[pl.BlockSpec((8, 256, 128), lambda i: (i, 0, 0))]
        + [
            whole(s)
            for s in (
                (512, 256),
                (2, 256),
                (2, 128),
                (1, 256),
                (256, 256),
                (256, 256),
                (256, 256),
                (256, 256),
                (1, 128),
                (128, 8),
                (1, 256),
                (256, 32),
            )
        ],
        out_specs=[whole((8, 176, 256)), whole((64, 256)), whole((2, 32, 256))],
        out_shape=[
            jax.ShapeDtypeStruct((8, 176, 256), BF16),
            jax.ShapeDtypeStruct((64, 256), F32),
            jax.ShapeDtypeStruct((2, 32, 256), BF16),
        ],
        scratch_shapes=[pltpu.VMEM((2, 256, 128), F32), pltpu.VMEM((2, 512, 128), F32)],
        compiler_params=params(),
    )(
        couple_activity,
        seq,
        live,
        position_valid_flags.reshape(2, 128),
        attend_scale_vector.reshape(1, 256),
        asking_matrix,
        lookup_matrix,
        content_matrix,
        sigmoid_matrix,
        couple_scale_vector.reshape(1, 128),
        headwise_additive_matrix,
        g2,
        other_factor_matrix,
    )

    heads = lax.all_to_all(message, "q", 0, 0, tiled=True)
    kv = heads[:, 32:176, :]
    own = heads[:, 160:176, 0:128]
    kva = lax.ppermute(kv, ("c", "x"), ACROSS)
    kvb = lax.ppermute(kv, ("c", "x"), ACROSS_NEXT)
    swapped = lax.ppermute(own, "x", SWAP)
    x0 = lax.ppermute(jnp.where(c == 0, right[0], right[1]), ALL, MIRROR)
    x1 = lax.ppermute(jnp.where(c == 0, right[1], right[0]), ALL, MIRROR_NEXT)
    bias = gather(heads[:, 0:32, :], "z", 8)

    parts = pl.pallas_call(
        attend_kernel,
        in_specs=[pl.BlockSpec(memory_space=pltpu.SMEM)] + [pl.BlockSpec(memory_space=pltpu.VMEM)] * 7,
        out_specs=pl.BlockSpec(memory_space=pltpu.VMEM),
        out_shape=jax.ShapeDtypeStruct((8, 2, 48, 256), BF16),
        scratch_shapes=[pltpu.VMEM((2, 128, 2048), F32)],
        compiler_params=params(),
    )(jnp.stack([c, x]).astype(jnp.int32), own, swapped, kva, kvb, bias, x0, x1)

    parts = lax.all_to_all(parts.reshape(16, 48, 256), ("q", "x"), 0, 0, tiled=True)
    mine = parts[:, 16:48, :]
    theirs = lax.ppermute(mine, "c", SWAP)

    fresh, sides = pl.pallas_call(
        refresh_kernel,
        in_specs=[pl.BlockSpec(memory_space=pltpu.VMEM)] * 8,
        out_specs=[pl.BlockSpec(memory_space=pltpu.VMEM)] * 2,
        out_shape=[jax.ShapeDtypeStruct((64, 256), BF16), jax.ShapeDtypeStruct((32, 128), BF16)],
        compiler_params=params(),
    )(parts, gate, prior, attend_final_matrix, g2, first_factor_matrix, other_factor_matrix, live_band)

    sides = gather(sides, ("z", "x"), 16).reshape(16, 32, 2, 2, 32)
    left = sides[:, :, :, 0].transpose(1, 0, 2, 3).reshape(1024, 32)
    right_band = lax.ppermute(sides[:, :, :, 1], ALL, MIRROR)
    right_band = right_band.transpose(1, 3, 0, 2).reshape(32, 1, 1024)
    even, odd = jnp.where(c == 0, mine, theirs), jnp.where(c == 0, theirs, mine)
    factors = jnp.stack([even.reshape(8, 2, 32, 256), odd.reshape(8, 2, 32, 256)], axis=1)
    factors = factors.transpose(4, 3, 0, 1, 2).reshape(32, 8, 1024)
    slot = lax.broadcasted_iota(jnp.int32, (1, 8, 1), 1)
    factors = jnp.where(slot == 0, right_band, factors).reshape(256, 1024)

    nvalid = jnp.sum(sequence_valid_flags.astype(F32))
    divisor = jnp.maximum(nvalid * positions.reshape(32, 8)[:, 0], 1.0)
    mapping = product_mapping_matrix.reshape(32, 4096)
    pair_out = pl.pallas_call(
        outer_kernel,
        grid=(4,),
        in_specs=[
            pl.BlockSpec(memory_space=pltpu.SMEM),
            whole((256, 1024)),
            pl.BlockSpec((256, 32), lambda i: (i, 0)),
            whole((32, 4096)),
            pl.BlockSpec((8, 256, 128), lambda i: (i, 0, 0)),
        ],
        out_specs=pl.BlockSpec((8, 256, 128), lambda i: (i, 0, 0)),
        out_shape=jax.ShapeDtypeStruct((32, 256, 128), BF16),
        scratch_shapes=[pltpu.VMEM((1024, 256), BF16)],
        compiler_params=params(),
    )(divisor, factors, left, mapping, couple_activity)
    return fresh.reshape(2, 32, 256), pair_out


def solution(mesh):
    mesh = Mesh(mesh.devices.reshape(8, 2, 8, 2), ALL)
    wide, narrow = ("q", "c"), ("z", "x")
    in_specs = (P(narrow, wide, None), P(wide, narrow, None), P(), P(wide)) + (P(),) * 12
    out_specs = (P(narrow, wide, None), P(wide, narrow, None))
    return jax.shard_map(local, mesh=mesh, in_specs=in_specs, out_specs=out_specs, check_vma=False)
```

```python
import jax
import jax.numpy as jnp
from jax import lax
from jax.experimental import pallas as pl
from jax.experimental.pallas import tpu as pltpu
from jax.sharding import Mesh, PartitionSpec as P

EPS = 1e-05
BIG = 1000000000.0
F32 = jnp.float32
BF16 = jnp.bfloat16
VMEM = 40 * 1024 * 1024
FULL = 60 * 1024 * 1024
ALL = ("q", "c", "z", "x")


def dot(a, b, dims):
    return lax.dot_general(a, b, (dims, ((), ())), preferred_element_type=F32)


NN = ((1,), (0,))
NT = ((1,), (1,))
TN = ((0,), (0,))
TT = ((0,), (1,))


def center_and_scale(values):
    center = values - jnp.mean(values, axis=-1, keepdims=True)
    spread = jnp.mean(center * center, axis=-1, keepdims=True)
    return center * lax.rsqrt(spread + EPS)


def row_of(flags, count):
    lane = lax.broadcasted_iota(jnp.int32, (count, 256), 1)
    row = lax.broadcasted_iota(jnp.int32, (count, 256), 0)
    return jnp.sum(jnp.where(lane == row * 8, flags, 0.0), axis=1, keepdims=True)


def front_kernel(
    live_ref,
    pair_ref,
    seq_ref,
    flags_ref,
    g1_ref,
    ask_ref,
    look_ref,
    cont_ref,
    sig_ref,
    gp_ref,
    head_ref,
    g2_ref,
    other_ref,
    msg_ref,
    gate_ref,
    prior_ref,
    right_ref,
    bias_scr,
    norm_scr,
):
    step = pl.program_id(0)
    rows = pair_ref.shape[0]
    first_row = (lax.axis_index("z") * 2 + lax.axis_index("x")) * 2

    pair = pair_ref[...].reshape(rows * 256, 128).astype(F32)
    pair = (center_and_scale(pair) * gp_ref[...]).astype(BF16)
    bias = dot(head_ref[...], pair, NT)
    for r in range(rows):
        for i in range(2):
            bias_scr[i, pl.ds(pl.multiple_of((step * rows + r) * 8, 8), 8), :] = bias[
                :, r * 256 + i * 128 : r * 256 + i * 128 + 128
            ]

    @pl.when(step == 0)
    def _():
        raw = seq_ref[...].astype(F32)
        base = center_and_scale(raw)
        normed = (base * g1_ref[...]).astype(BF16)
        keys = dot(look_ref[...], normed, TT).astype(BF16)
        values = dot(cont_ref[...], normed, TT).astype(BF16)
        for h in range(8):
            for s in range(2):
                cut = (slice(h * 32, h * 32 + 32), slice(s * 256, s * 256 + 256))
                msg_ref[h, 32 + s * 32 : 64 + s * 32, :] = keys[cut]
                msg_ref[h, 96 + s * 32 : 128 + s * 32, :] = values[cut]
        wide = normed.astype(F32)
        for i in range(2):
            norm_scr[i] = wide[:, i * 128 : (i + 1) * 128]
            norm_scr[2 + i] = raw[:, i * 128 : (i + 1) * 128]
        cuts = [norm_scr[i, pl.ds(0, 64, stride=8), :] for i in range(4)]
        band = jnp.concatenate(cuts[:2], axis=1).astype(BF16)
        prior_ref[...] = jnp.concatenate(cuts[2:], axis=1)
        gate_ref[...] = jax.nn.sigmoid(dot(band, sig_ref[...], NN))
        query = (dot(band, ask_ref[...], NN) * 32 ** (-0.5)).astype(BF16).astype(F32)
        flags = flags_ref[...].astype(F32)
        row = lax.broadcasted_iota(jnp.int32, (16, 128), 0)
        mask = jnp.where(row == 0, flags[0:1], jnp.where(row == 1, flags[1:2], 0.0))
        for h in range(8):
            parts = [
                query[s * 32 + g * 16 : s * 32 + g * 16 + 16, h * 32 : h * 32 + 32]
                for g in range(2)
                for s in range(2)
            ]
            msg_ref[h, 160:176, :] = jnp.concatenate(parts + [mask], axis=1).astype(BF16)
        again = (base * g2_ref[...]).astype(BF16)
        right = dot(other_ref[...], again, NT)
        flags = jnp.concatenate([flags[0:1], flags[1:2]], axis=1)
        for s in range(2):
            live = live_ref[first_row + s].astype(F32) * flags
            right_ref[s] = (right[:, s * 256 : (s + 1) * 256] * live).astype(BF16)

    @pl.when(step == pl.num_programs(0) - 1)
    def _():
        for h in range(8):
            for i in range(2):
                msg_ref[h, 0:32, i * 128 : i * 128 + 128] = bias_scr[
                    i, pl.ds(h, 32, stride=8), :
                ].astype(BF16)


def split3(value):
    high = value.astype(BF16).astype(F32)
    rest = value - high
    middle = rest.astype(BF16).astype(F32)
    return high, middle, rest - middle


def attend_kernel(
    own_ref, swapped_ref, kva_ref, kvb_ref, bias_ref, x0_ref, x1_ref, out_ref, extra_scr
):
    c, x = lax.axis_index("c"), lax.axis_index("x")
    lane = lax.broadcasted_iota(jnp.int32, (128, 128), 1)
    block, inner = lane // 32, lane % 32
    first_x = jnp.where(x == 0, x0_ref[...], x1_ref[...])
    second_x = jnp.where(x == 0, x1_ref[...], x0_ref[...])
    for q in range(8):
        out_ref[q, 0, 16:48, :] = first_x
        out_ref[q, 1, 16:48, :] = second_x
    mask = jnp.concatenate(
        [kva_ref[k, 128 + i : 129 + i, 128:256].astype(F32) for k in range(8) for i in range(2)], axis=1
    )
    penalty = BIG * (mask - 1.0)
    for g in range(2):
        for k in range(8):
            piece = bias_ref[k, :, g * 16 : g * 16 + 16, :].reshape(128, 256).astype(F32)
            extra_scr[g, :, k * 256 : (k + 1) * 256] = piece + penalty[:, k * 256 : (k + 1) * 256]
    own = own_ref[...].reshape(128, 128)
    swapped = swapped_ref[...].reshape(128, 128)
    for a in range(2):
        kv_ref = (kva_ref, kvb_ref)[a]
        half = c ^ a
        query = jnp.where(half == x, own, swapped).astype(F32)
        keys = jnp.concatenate([kv_ref[k, 0:64, :] for k in range(8)], axis=1)
        values = jnp.concatenate([kv_ref[k, 64:128, :] for k in range(8)], axis=1)
        keys = jnp.concatenate([keys, keys], axis=0)
        values = jnp.concatenate([values, values], axis=0)
        mixed = jnp.zeros((128, 128), F32)
        stats = jnp.zeros((128, 128), F32)
        for g in range(2):
            for s in range(2):
                here = block == g * 2 + s
                picked = jnp.where(here, query, 0.0).astype(BF16)
                scores = dot(picked, keys, NN) + extra_scr[g]
                top = jnp.max(scores, axis=1, keepdims=True)
                expo = jnp.exp(scores - top)
                total = jnp.sum(expo, axis=1, keepdims=True)
                part = dot(expo.astype(BF16), values, NT)
                mixed = jnp.where(here, part / total, mixed)
                for t, piece in enumerate(split3(top) + split3(total)):
                    stats = jnp.where(here & (inner == t), piece, stats)
        joined = jnp.concatenate([mixed, stats], axis=1).astype(BF16)
        for q in range(8):
            out_ref[q, half, 0:16, :] = joined[q * 16 : q * 16 + 16]


def refresh_kernel(
    live_ref,
    parts_ref,
    gate_ref,
    prior_ref,
    flags_ref,
    final_ref,
    g2_ref,
    first_ref,
    other_ref,
    fresh_ref,
    sides_ref,
):
    first_row = (lax.axis_index("z") * 2 + lax.axis_index("x")) * 2
    flags = flags_ref[...].astype(F32)
    band = row_of(jnp.concatenate([flags[0:1], flags[1:2]], axis=1), 32)
    live = jnp.concatenate([band * live_ref[first_row + s].astype(F32) for s in range(2)], axis=0)
    rows = lax.broadcasted_iota(jnp.int32, (128, 128), 0)
    lanes = lax.broadcasted_iota(jnp.int32, (128, 128), 1)
    spread = [jnp.where(rows == (lanes // 32) * 32 + t, 1.0, 0.0).astype(BF16) for t in range(6)]
    tops, totals, mixes = [], [], []
    for x in range(2):
        mixes.append(
            jnp.concatenate([parts_ref[2 * h + x, 0:16, 0:128] for h in range(8)], axis=0).astype(F32)
        )
        stats = jnp.concatenate([parts_ref[2 * h + x, 0:16, 128:256] for h in range(8)], axis=0)
        wide = [dot(stats, spread[t], NN) for t in range(6)]
        tops.append(wide[0] + wide[1] + wide[2])
        totals.append(wide[3] + wide[4] + wide[5])
    top = jnp.maximum(tops[0], tops[1])
    weights = [totals[i] * jnp.exp(tops[i] - top) for i in range(2)]
    attended = (weights[0] * mixes[0] + weights[1] * mixes[1]) / (weights[0] + weights[1])
    lined = []
    for s in range(2):
        for g in range(2):
            cut = (g * 2 + s) * 32
            lined.append(
                jnp.concatenate(
                    [attended[h * 16 : h * 16 + 16, cut : cut + 32] for h in range(8)], axis=1
                )
            )
    attended = jnp.concatenate(lined, axis=0)
    gated = (gate_ref[...] * attended).astype(BF16)
    fresh = (prior_ref[...] + dot(gated, final_ref[...], NN)).astype(BF16)
    fresh_ref[...] = fresh
    again = (center_and_scale(fresh.astype(F32)) * g2_ref[...]).astype(BF16)
    for i, factor in enumerate((first_ref, other_ref)):
        side = dot(again, factor[...], NT) * live
        parts = [side[s * 32 + g * 16 : s * 32 + g * 16 + 16] for g in range(2) for s in range(2)]
        sides_ref[i * 16 : i * 16 + 16, :] = jnp.concatenate(parts, axis=1).astype(BF16)


def pack_kernel(mine_ref, theirs_ref, map_ref, factors_ref, mapping_ref, scr):
    swapped = lax.axis_index("c") == 1
    rows = []
    for q in range(8):
        for c in range(2):
            for x in range(2):
                mine = mine_ref[2 * q + x, 16:48, :].astype(F32)
                theirs = theirs_ref[2 * q + x].astype(F32)
                rows.append(jnp.where(swapped == (c == 1), mine, theirs))
    for i in range(8):
        factors_ref[:, i * 128 : (i + 1) * 128] = jnp.concatenate(
            rows[i * 4 : i * 4 + 4], axis=0
        ).T.astype(BF16)
    scr[...] = map_ref[...].astype(F32)
    for d in range(32):
        piece = scr[pl.ds(d, 32, stride=32), :].astype(BF16)
        for k in range(4):
            mapping_ref[k * 32 : k * 32 + 32, d * 128 : (d + 1) * 128] = piece


def map_kernel(sides_ref, mapping_ref, out_ref, side_scr, scr):
    step = pl.program_id(0)

    @pl.when(step == 0)
    def _():
        for n in range(16):
            side_scr[n * 16 : n * 16 + 16, :] = sides_ref[n, 0:16, :].astype(F32)

    block = lax.broadcasted_iota(jnp.int32, (16, 128), 1) // 32
    group = step // 2
    lefts = []
    for r in range(8):
        lined = side_scr[pl.ds((step % 2) * 8 + r, 16, stride=16), :]
        for s in range(2):
            lefts.append(jnp.where(block == group * 2 + s, lined, 0.0))
    left = jnp.concatenate(lefts, axis=0).astype(BF16)
    for d in range(0, 32, 2):
        mapped = dot(left, mapping_ref[:, d * 128 : (d + 2) * 128], NN)
        for e in range(2):
            for r in range(8):
                for s in range(2):
                    scr[r, pl.ds(s * 32 + d + e, 16, stride=64), :] = mapped[
                        r * 32 + s * 16 : r * 32 + s * 16 + 16, e * 128 : e * 128 + 128
                    ]
    for r in range(8):
        out_ref[r // 2, :, (r % 2) * 128 : (r % 2) * 128 + 128] = scr[r].astype(BF16)


def outer_kernel(live_ref, flags_ref, factors_ref, band_ref, mapped_ref, pair_ref, out_ref, scr, full_scr):
    step = pl.program_id(0)
    rows = pair_ref.shape[0]

    @pl.when(step == 0)
    def _():
        for i in range(8):
            scr[...] = factors_ref[:, i * 128 : (i + 1) * 128].astype(F32)
            pair = [band_ref[2 * i + n].astype(F32) for n in range(2)]
            band = jnp.concatenate(
                [jnp.concatenate([p[:, g * 64 : g * 64 + 64] for p in pair], axis=1) for g in range(2)], axis=0
            )
            scr[pl.ds(0, 32, stride=8), :] = band
            full_scr[:, i * 128 : (i + 1) * 128] = scr[...].astype(BF16)

    nvalid = jnp.int32(0)
    for s in range(32):
        nvalid += live_ref[s]
    for r in range(0, rows, 2):
        projected = dot(full_scr[...], mapped_ref[r // 2], NN)
        for i in range(2):
            flag = flags_ref[(step * rows + r + i) * 8]
            scale = 1.0 / jnp.maximum((nvalid * flag).astype(F32), 1.0)
            out_ref[r + i] = (
                pair_ref[r + i].astype(F32) + projected[:, i * 128 : (i + 1) * 128] * scale
            ).astype(BF16)


def gather(value, axes, count):
    tiled = jnp.broadcast_to(value[None], (count,) + value.shape)
    return lax.all_to_all(tiled, axes, 0, 0, tiled=True)


def whole(shape):
    return pl.BlockSpec(shape, lambda *_: (0,) * len(shape))


SCALARS = pl.BlockSpec(memory_space=pltpu.SMEM)
ARRAY = pl.BlockSpec(memory_space=pltpu.VMEM)


def params():
    return pltpu.CompilerParams(vmem_limit_bytes=VMEM)


MIRROR = [(w * 16 + n, n * 16 + w) for w in range(16) for n in range(16)]
MIRROR_NEXT = [(w * 16 + n, n * 16 + (w ^ 1)) for w in range(16) for n in range(16)]
ACROSS = [(a * 2 + b, b * 2 + a) for a in range(2) for b in range(2)]
ACROSS_NEXT = [(a * 2 + b, (1 - b) * 2 + a) for a in range(2) for b in range(2)]
SWAP = [(0, 1), (1, 0)]


def local(
    sequence_activity,
    couple_activity,
    sequence_valid_flags,
    position_valid_flags,
    attend_scale_vector,
    asking_matrix,
    lookup_matrix,
    content_matrix,
    sigmoid_matrix,
    attend_final_matrix,
    couple_scale_vector,
    headwise_additive_matrix,
    product_scale_vector,
    first_factor_matrix,
    other_factor_matrix,
    product_mapping_matrix,
):
    c = lax.axis_index("c")
    g2 = product_scale_vector.reshape(1, 256)
    flags = position_valid_flags.reshape(2, 128)
    first, other = first_factor_matrix.T, other_factor_matrix.T

    message, gate, prior, right = pl.pallas_call(
        front_kernel,
        grid=(4,),
        in_specs=[SCALARS, pl.BlockSpec((8, 256, 128), lambda i: (i, 0, 0))]
        + [
            whole(s)
            for s in (
                (512, 256),
                (2, 128),
                (1, 256),
                (256, 256),
                (256, 256),
                (256, 256),
                (256, 256),
                (1, 128),
                (8, 128),
                (1, 256),
                (32, 256),
            )
        ],
        out_specs=[whole((8, 176, 256)), whole((64, 256)), whole((64, 256)), whole((2, 32, 256))],
        out_shape=[
            jax.ShapeDtypeStruct((8, 176, 256), BF16),
            jax.ShapeDtypeStruct((64, 256), F32),
            jax.ShapeDtypeStruct((64, 256), F32),
            jax.ShapeDtypeStruct((2, 32, 256), BF16),
        ],
        scratch_shapes=[pltpu.VMEM((2, 256, 128), F32), pltpu.VMEM((4, 512, 128), F32)],
        compiler_params=pltpu.CompilerParams(vmem_limit_bytes=FULL),
    )(
        sequence_valid_flags,
        couple_activity,
        sequence_activity.reshape(512, 256),
        flags,
        attend_scale_vector.reshape(1, 256),
        asking_matrix,
        lookup_matrix,
        content_matrix,
        sigmoid_matrix,
        couple_scale_vector.reshape(1, 128),
        headwise_additive_matrix.T,
        g2,
        other,
    )

    heads = lax.all_to_all(message, "q", 0, 0, tiled=True)
    kv = heads[:, 32:176, :]
    own = heads[:, 160:176, 0:128]
    kva = lax.ppermute(kv, ("c", "x"), ACROSS)
    kvb = lax.ppermute(kv, ("c", "x"), ACROSS_NEXT)
    swapped = lax.ppermute(own, "x", SWAP)
    x0 = lax.ppermute(jnp.where(c == 0, right[0], right[1]), ALL, MIRROR)
    x1 = lax.ppermute(jnp.where(c == 0, right[1], right[0]), ALL, MIRROR_NEXT)
    bias = gather(heads[:, 0:32, :], "z", 8)

    parts = pl.pallas_call(
        attend_kernel,
        in_specs=[ARRAY] * 7,
        out_specs=ARRAY,
        out_shape=jax.ShapeDtypeStruct((8, 2, 48, 256), BF16),
        scratch_shapes=[pltpu.VMEM((2, 128, 2048), F32)],
        compiler_params=params(),
    )(own, swapped, kva, kvb, bias, x0, x1)

    parts = lax.all_to_all(parts.reshape(16, 48, 256), ("q", "x"), 0, 0, tiled=True)
    theirs = lax.ppermute(parts[:, 16:48, :], "c", SWAP)

    fresh, sides = pl.pallas_call(
        refresh_kernel,
        in_specs=[SCALARS] + [ARRAY] * 8,
        out_specs=[ARRAY] * 2,
        out_shape=[jax.ShapeDtypeStruct((64, 256), BF16), jax.ShapeDtypeStruct((32, 128), BF16)],
        compiler_params=params(),
    )(sequence_valid_flags, parts, gate, prior, flags, attend_final_matrix, g2, first, other)

    sides = gather(sides, ("z", "x"), 16)
    band = lax.ppermute(sides[:, 16:32, :], ALL, MIRROR)

    factors, mapping = pl.pallas_call(
        pack_kernel,
        in_specs=[ARRAY] * 3,
        out_specs=[ARRAY] * 2,
        out_shape=[jax.ShapeDtypeStruct((256, 1024), BF16), jax.ShapeDtypeStruct((128, 4096), BF16)],
        scratch_shapes=[pltpu.VMEM((1024, 128), F32)],
        cost_estimate=pl.CostEstimate(flops=0, bytes_accessed=12 << 20, transcendentals=0),
        compiler_params=params(),
    )(parts, theirs, product_mapping_matrix)
    mapped = pl.pallas_call(
        map_kernel,
        grid=(4,),
        in_specs=[whole((16, 32, 128)), whole((128, 4096))],
        out_specs=pl.BlockSpec((4, 1024, 256), lambda i: (i, 0, 0)),
        out_shape=jax.ShapeDtypeStruct((16, 1024, 256), BF16),
        scratch_shapes=[pltpu.VMEM((256, 128), F32), pltpu.VMEM((8, 1024, 128), F32)],
        cost_estimate=pl.CostEstimate(flops=4 << 30, bytes_accessed=20 << 20, transcendentals=0),
        compiler_params=params(),
    )(sides, mapping)
    pair_out = pl.pallas_call(
        outer_kernel,
        grid=(4,),
        in_specs=[
            SCALARS,
            SCALARS,
            whole((256, 1024)),
            whole((16, 16, 128)),
            pl.BlockSpec((4, 1024, 256), lambda i: (i, 0, 0)),
            pl.BlockSpec((8, 256, 128), lambda i: (i, 0, 0)),
        ],
        out_specs=pl.BlockSpec((8, 256, 128), lambda i: (i, 0, 0)),
        out_shape=jax.ShapeDtypeStruct((32, 256, 128), BF16),
        scratch_shapes=[pltpu.VMEM((256, 128), F32), pltpu.VMEM((256, 1024), BF16)],
        compiler_params=params(),
    )(sequence_valid_flags, position_valid_flags, factors, band, mapped, couple_activity)
    return fresh.reshape(2, 32, 256), pair_out


def solution(mesh):
    mesh = Mesh(mesh.devices.reshape(8, 2, 8, 2), ALL)
    wide, narrow = ("q", "c"), ("z", "x")
    in_specs = (P(narrow, wide, None), P(wide, narrow, None), P(), P(wide)) + (P(),) * 12
    out_specs = (P(narrow, wide, None), P(wide, narrow, None))
    return jax.shard_map(local, mesh=mesh, in_specs=in_specs, out_specs=out_specs, check_vma=False)
```

```python
import jax
import jax.numpy as jnp
from jax import lax
from jax.experimental import pallas as pl
from jax.experimental.pallas import tpu as pltpu
from jax.sharding import Mesh, PartitionSpec as P

EPS = 1e-05
BIG = 1000000000.0
F32 = jnp.float32
BF16 = jnp.bfloat16
VMEM = 40 * 1024 * 1024
FULL = 60 * 1024 * 1024
ALL = ("q", "c", "z", "x")


def dot(a, b, dims):
    return lax.dot_general(a, b, (dims, ((), ())), preferred_element_type=F32)


NN = ((1,), (0,))
NT = ((1,), (1,))
TN = ((0,), (0,))
TT = ((0,), (1,))


def center_and_scale(values):
    center = values - jnp.mean(values, axis=-1, keepdims=True)
    spread = jnp.mean(center * center, axis=-1, keepdims=True)
    return center * lax.rsqrt(spread + EPS)


def row_of(flags, count):
    lane = lax.broadcasted_iota(jnp.int32, (count, 256), 1)
    row = lax.broadcasted_iota(jnp.int32, (count, 256), 0)
    return jnp.sum(jnp.where(lane == row * 8, flags, 0.0), axis=1, keepdims=True)


def front_kernel(
    live_ref,
    pair_ref,
    seq_ref,
    flags_ref,
    g1_ref,
    ask_ref,
    look_ref,
    cont_ref,
    sig_ref,
    gp_ref,
    head_ref,
    g2_ref,
    other_ref,
    msg_ref,
    gate_ref,
    prior_ref,
    right_ref,
    bias_scr,
    norm_scr,
):
    step = pl.program_id(0)
    rows = pair_ref.shape[0]
    first_row = (lax.axis_index("z") * 2 + lax.axis_index("x")) * 2

    pair = pair_ref[...].reshape(rows * 256, 128).astype(F32)
    pair = (center_and_scale(pair) * gp_ref[...]).astype(BF16)
    bias = dot(head_ref[...], pair, NT)
    for r in range(rows):
        for i in range(2):
            bias_scr[i, pl.ds(pl.multiple_of((step * rows + r) * 8, 8), 8), :] = bias[
                :, r * 256 + i * 128 : r * 256 + i * 128 + 128
            ]

    @pl.when(step == 0)
    def _():
        raw = seq_ref[...].astype(F32)
        base = center_and_scale(raw)
        normed = (base * g1_ref[...]).astype(BF16)
        keys = dot(look_ref[...], normed, TT).astype(BF16)
        values = dot(cont_ref[...], normed, TT).astype(BF16)
        for h in range(8):
            for s in range(2):
                cut = (slice(h * 32, h * 32 + 32), slice(s * 256, s * 256 + 256))
                msg_ref[h, 32 + s * 32 : 64 + s * 32, :] = keys[cut]
                msg_ref[h, 96 + s * 32 : 128 + s * 32, :] = values[cut]
        wide = normed.astype(F32)
        for i in range(2):
            norm_scr[i] = wide[:, i * 128 : (i + 1) * 128]
            norm_scr[2 + i] = raw[:, i * 128 : (i + 1) * 128]
        cuts = [norm_scr[i, pl.ds(0, 64, stride=8), :] for i in range(4)]
        band = jnp.concatenate(cuts[:2], axis=1).astype(BF16)
        prior_ref[...] = jnp.concatenate(cuts[2:], axis=1)
        gate_ref[...] = jax.nn.sigmoid(dot(band, sig_ref[...], NN))
        query = (dot(band, ask_ref[...], NN) * 32 ** (-0.5)).astype(BF16).astype(F32)
        flags = flags_ref[...].astype(F32)
        row = lax.broadcasted_iota(jnp.int32, (16, 128), 0)
        mask = jnp.where(row == 0, flags[0:1], jnp.where(row == 1, flags[1:2], 0.0))
        for h in range(8):
            parts = [
                query[s * 32 + g * 16 : s * 32 + g * 16 + 16, h * 32 : h * 32 + 32]
                for g in range(2)
                for s in range(2)
            ]
            msg_ref[h, 160:176, :] = jnp.concatenate(parts + [mask], axis=1).astype(BF16)
        again = (base * g2_ref[...]).astype(BF16)
        right = dot(other_ref[...], again, NT)
        flags = jnp.concatenate([flags[0:1], flags[1:2]], axis=1)
        for s in range(2):
            live = live_ref[first_row + s].astype(F32) * flags
            right_ref[s] = (right[:, s * 256 : (s + 1) * 256] * live).astype(BF16)

    @pl.when(step == pl.num_programs(0) - 1)
    def _():
        for h in range(8):
            for i in range(2):
                msg_ref[h, 0:32, i * 128 : i * 128 + 128] = bias_scr[
                    i, pl.ds(h, 32, stride=8), :
                ].astype(BF16)


def split3(value):
    high = value.astype(BF16).astype(F32)
    rest = value - high
    middle = rest.astype(BF16).astype(F32)
    return high, middle, rest - middle


def attend_blocks(own_ref, swapped_ref, kva_ref, kvb_ref, blocks, extra_scr):
    c, x, z = lax.axis_index("c"), lax.axis_index("x"), lax.axis_index("z")
    places = [lax.rem(z + offset + 8, 8) for offset, _ in blocks]
    block = lax.broadcasted_iota(jnp.int32, (128, 128), 1) // 32
    for k, (place, (_, bias_ref)) in enumerate(zip(places, blocks)):
        mask = jnp.concatenate(
            [kva_ref[place, 128 + i : 129 + i, 128:256].astype(F32) for i in range(2)], axis=1
        )
        for g in range(2):
            piece = bias_ref[:, g * 16 : g * 16 + 16, :].reshape(128, 256).astype(F32)
            extra_scr[g, :, k * 256 : (k + 1) * 256] = piece + BIG * (mask - 1.0)
    own = own_ref[...].reshape(128, 128)
    swapped = swapped_ref[...].reshape(128, 128)
    states = []
    for a, kv_ref in enumerate((kva_ref, kvb_ref)):
        query = jnp.where((c ^ a) == x, own, swapped).astype(F32)
        keys = jnp.concatenate([kv_ref[place, 0:64, :] for place in places], axis=1)
        values = jnp.concatenate([kv_ref[place, 64:128, :] for place in places], axis=1)
        keys = jnp.concatenate([keys, keys], axis=0)
        values = jnp.concatenate([values, values], axis=0)
        state = [jnp.zeros((128, 128), F32)] * 3
        for g in range(2):
            for s in range(2):
                here = block == g * 2 + s
                picked = jnp.where(here, query, 0.0).astype(BF16)
                scores = dot(picked, keys, NN) + extra_scr[g]
                top = jnp.max(scores, axis=1, keepdims=True)
                expo = jnp.exp(scores - top)
                total = jnp.sum(expo, axis=1, keepdims=True)
                mixed = dot(expo.astype(BF16), values, NT)
                state = [jnp.where(here, new, old) for new, old in zip((mixed, top, total), state)]
        states.append(state)
    return states


def attend_kernel(own_ref, swapped_ref, kva_ref, kvb_ref, *refs):
    *bias_refs, out_ref, extra_scr = refs
    blocks = list(zip((0, -1, 1, -2, 2), bias_refs))
    states = attend_blocks(own_ref, swapped_ref, kva_ref, kvb_ref, blocks, extra_scr)
    for a in range(2):
        for i in range(3):
            out_ref[a, i] = states[a][i]


def finish_kernel(own_ref, swapped_ref, kva_ref, kvb_ref, *refs):
    *bias_refs, state_ref, x0_ref, x1_ref, out_ref, extra_scr = refs
    c, x = lax.axis_index("c"), lax.axis_index("x")
    for q in range(8):
        out_ref[q, x, 16:48, :] = x0_ref[x]
        out_ref[q, 1 - x, 16:48, :] = x1_ref[x]
    inner = lax.broadcasted_iota(jnp.int32, (128, 128), 1) % 32
    blocks = list(zip((-3, 3, -4), bias_refs))
    states = attend_blocks(own_ref, swapped_ref, kva_ref, kvb_ref, blocks, extra_scr)
    for a in range(2):
        mixed, top, total = states[a]
        other_mixed, other_top, other_total = (state_ref[a, i] for i in range(3))
        best = jnp.maximum(top, other_top)
        weight, other_weight = jnp.exp(top - best), jnp.exp(other_top - best)
        total = total * weight + other_total * other_weight
        mixed = (mixed * weight + other_mixed * other_weight) / total
        stats = jnp.zeros((128, 128), F32)
        for t, piece in enumerate(split3(best) + split3(total)):
            stats = jnp.where(inner == t, piece, stats)
        joined = jnp.concatenate([mixed, stats], axis=1).astype(BF16)
        for q in range(8):
            out_ref[q, c ^ a, 0:16, :] = joined[q * 16 : q * 16 + 16]


def refresh_kernel(
    live_ref,
    parts_ref,
    gate_ref,
    prior_ref,
    flags_ref,
    final_ref,
    g2_ref,
    first_ref,
    other_ref,
    fresh_ref,
    sides_ref,
):
    first_row = (lax.axis_index("z") * 2 + lax.axis_index("x")) * 2
    flags = flags_ref[...].astype(F32)
    band = row_of(jnp.concatenate([flags[0:1], flags[1:2]], axis=1), 32)
    live = jnp.concatenate([band * live_ref[first_row + s].astype(F32) for s in range(2)], axis=0)
    rows = lax.broadcasted_iota(jnp.int32, (128, 128), 0)
    lanes = lax.broadcasted_iota(jnp.int32, (128, 128), 1)
    spread = [jnp.where(rows == (lanes // 32) * 32 + t, 1.0, 0.0).astype(BF16) for t in range(6)]
    tops, totals, mixes = [], [], []
    for x in range(2):
        mixes.append(
            jnp.concatenate([parts_ref[2 * h + x, 0:16, 0:128] for h in range(8)], axis=0).astype(F32)
        )
        stats = jnp.concatenate([parts_ref[2 * h + x, 0:16, 128:256] for h in range(8)], axis=0)
        wide = [dot(stats, spread[t], NN) for t in range(6)]
        tops.append(wide[0] + wide[1] + wide[2])
        totals.append(wide[3] + wide[4] + wide[5])
    top = jnp.maximum(tops[0], tops[1])
    weights = [totals[i] * jnp.exp(tops[i] - top) for i in range(2)]
    attended = (weights[0] * mixes[0] + weights[1] * mixes[1]) / (weights[0] + weights[1])
    lined = []
    for s in range(2):
        for g in range(2):
            cut = (g * 2 + s) * 32
            lined.append(
                jnp.concatenate(
                    [attended[h * 16 : h * 16 + 16, cut : cut + 32] for h in range(8)], axis=1
                )
            )
    attended = jnp.concatenate(lined, axis=0)
    gated = (gate_ref[...] * attended).astype(BF16)
    fresh = (prior_ref[...] + dot(gated, final_ref[...], NN)).astype(BF16)
    fresh_ref[...] = fresh
    again = (center_and_scale(fresh.astype(F32)) * g2_ref[...]).astype(BF16)
    for i, factor in enumerate((first_ref, other_ref)):
        side = dot(again, factor[...], NT) * live
        parts = [side[s * 32 + g * 16 : s * 32 + g * 16 + 16] for g in range(2) for s in range(2)]
        sides_ref[i * 16 : i * 16 + 16, :] = jnp.concatenate(parts, axis=1).astype(BF16)


def pack_kernel(mine_ref, theirs_ref, factors_ref, factor_scr):
    swapped = lax.axis_index("c") == 1
    for q in range(8):
        for c in range(2):
            for x in range(2):
                mine = mine_ref[2 * q + x, 16:48, :].astype(F32)
                theirs = theirs_ref[2 * q + x].astype(F32)
                piece = jnp.where(swapped == (c == 1), mine, theirs)
                place = (x * 16 + 2 * q + c) * 32
                for i in range(2):
                    factor_scr[i, place : place + 32, :] = piece[:, i * 128 : i * 128 + 128]
    for k in range(8):
        rows = []
        for d in range(k * 4, k * 4 + 4):
            rows.append(
                jnp.concatenate([factor_scr[i, pl.ds(d, 32, stride=32), :] for i in range(2)], axis=1)
            )
        factors_ref[:, k * 128 : (k + 1) * 128] = jnp.concatenate(rows, axis=0).T.astype(BF16)


def line_kernel(map_ref, mapping_ref, scr):
    scr[...] = map_ref[...].astype(F32)
    for d in range(32):
        piece = scr[pl.ds(d, 32, stride=32), :].astype(BF16)
        for k in range(4):
            mapping_ref[k * 32 : k * 32 + 32, d * 128 : (d + 1) * 128] = piece


def map_kernel(sides_ref, mapping_ref, out_ref, side_scr):
    step = pl.program_id(0)

    @pl.when(step == 0)
    def _():
        for n in range(16):
            side_scr[n * 16 : n * 16 + 16, :] = sides_ref[n, 0:16, :].astype(F32)

    block = lax.broadcasted_iota(jnp.int32, (16, 128), 1) // 32
    group = step // 2
    lefts = []
    for r in range(8):
        lined = side_scr[pl.ds((step % 2) * 8 + r, 16, stride=16), :]
        for s in range(2):
            lefts.append(jnp.where(block == group * 2 + s, lined, 0.0))
    left = jnp.concatenate(lefts, axis=0).astype(BF16)
    for d in range(0, 32, 2):
        mapped = dot(left, mapping_ref[:, d * 128 : (d + 2) * 128], NN).astype(BF16)
        for e in range(2):
            for r in range(8):
                out_ref[r // 2, (d + e) * 32 : (d + e) * 32 + 32, (r % 2) * 128 : (r % 2) * 128 + 128] = (
                    mapped[r * 32 : r * 32 + 32, e * 128 : e * 128 + 128]
                )


def outer_kernel(
    live_ref,
    flags_ref,
    factors_ref,
    band_ref,
    mapped_ref,
    pair_ref,
    out_ref,
    scr,
    band_scr,
    full_scr,
    done_scr,
    sems,
):
    turned = jnp.concatenate([band_ref[n].astype(F32) for n in range(16)], axis=0).T
    empty = jnp.zeros((32, 96), F32)
    for s in range(2):
        for n in range(16):
            parts = [
                turned[g * 64 + s * 32 : g * 64 + s * 32 + 32, n * 16 : n * 16 + 16] for g in range(2)
            ]
            band_scr[pl.ds(s * 16 + n, 32, stride=32), :] = jnp.concatenate(parts + [empty], axis=1)
    for i in range(8):
        scr[i] = factors_ref[:, i * 128 : (i + 1) * 128].astype(F32)
        scr[i, pl.ds(0, 32, stride=8), :] = band_scr[i * 128 : (i + 1) * 128, :].T[0:32]
        full_scr[:, i * 128 : (i + 1) * 128] = scr[i].astype(BF16)

    nvalid = jnp.int32(0)
    for s in range(32):
        nvalid += live_ref[s]
    copies = []
    for k in range(8):
        for r in range(k * 4, k * 4 + 4, 2):
            projected = dot(full_scr[...], mapped_ref[r // 2], NN)
            for i in range(2):
                scale = 1.0 / jnp.maximum((nvalid * flags_ref[(r + i) * 8]).astype(F32), 1.0)
                done_scr[r + i] = (
                    pair_ref[r + i].astype(F32) + projected[:, i * 128 : (i + 1) * 128] * scale
                ).astype(BF16)
        part = pl.ds(k * 4, 4)
        copies.append(pltpu.make_async_copy(done_scr.at[part], out_ref.at[part], sems.at[k]))
        copies[-1].start()
    for copy in copies:
        copy.wait()


def gather(value, axes, count):
    tiled = jnp.broadcast_to(value[None], (count,) + value.shape)
    return lax.all_to_all(tiled, axes, 0, 0, tiled=True)


def whole(shape):
    return pl.BlockSpec(shape, lambda *_: (0,) * len(shape))


SCALARS = pl.BlockSpec(memory_space=pltpu.SMEM)
ARRAY = pl.BlockSpec(memory_space=pltpu.VMEM)


def params():
    return pltpu.CompilerParams(vmem_limit_bytes=VMEM)


MIRROR = [(w * 16 + n, n * 16 + w) for w in range(16) for n in range(16)]
ACROSS = [(a * 2 + b, b * 2 + a) for a in range(2) for b in range(2)]
ACROSS_NEXT = [(a * 2 + b, (1 - b) * 2 + a) for a in range(2) for b in range(2)]
SWAP = [(0, 1), (1, 0)]
UP = [(i, (i + 1) % 8) for i in range(8)]
DOWN = [(i, (i + 7) % 8) for i in range(8)]


def local(
    sequence_activity,
    couple_activity,
    sequence_valid_flags,
    position_valid_flags,
    attend_scale_vector,
    asking_matrix,
    lookup_matrix,
    content_matrix,
    sigmoid_matrix,
    attend_final_matrix,
    couple_scale_vector,
    headwise_additive_matrix,
    product_scale_vector,
    first_factor_matrix,
    other_factor_matrix,
    product_mapping_matrix,
):
    g2 = product_scale_vector.reshape(1, 256)
    flags = position_valid_flags.reshape(2, 128)
    first, other = first_factor_matrix.T, other_factor_matrix.T

    message, gate, prior, right = pl.pallas_call(
        front_kernel,
        grid=(4,),
        in_specs=[SCALARS, pl.BlockSpec((8, 256, 128), lambda i: (i, 0, 0))]
        + [
            whole(s)
            for s in (
                (512, 256),
                (2, 128),
                (1, 256),
                (256, 256),
                (256, 256),
                (256, 256),
                (256, 256),
                (1, 128),
                (8, 128),
                (1, 256),
                (32, 256),
            )
        ],
        out_specs=[whole((8, 176, 256)), whole((64, 256)), whole((64, 256)), whole((2, 32, 256))],
        out_shape=[
            jax.ShapeDtypeStruct((8, 176, 256), BF16),
            jax.ShapeDtypeStruct((64, 256), F32),
            jax.ShapeDtypeStruct((64, 256), F32),
            jax.ShapeDtypeStruct((2, 32, 256), BF16),
        ],
        scratch_shapes=[pltpu.VMEM((2, 256, 128), F32), pltpu.VMEM((4, 512, 128), F32)],
        compiler_params=pltpu.CompilerParams(vmem_limit_bytes=FULL),
    )(
        sequence_valid_flags,
        couple_activity,
        sequence_activity.reshape(512, 256),
        flags,
        attend_scale_vector.reshape(1, 256),
        asking_matrix,
        lookup_matrix,
        content_matrix,
        sigmoid_matrix,
        couple_scale_vector.reshape(1, 128),
        headwise_additive_matrix.T,
        g2,
        other,
    )

    heads = lax.all_to_all(message, "q", 0, 0, tiled=True)
    x0 = lax.ppermute(right, ALL, MIRROR)
    mapping = pl.pallas_call(
        line_kernel,
        in_specs=[ARRAY],
        out_specs=ARRAY,
        out_shape=jax.ShapeDtypeStruct((128, 4096), BF16),
        scratch_shapes=[pltpu.VMEM((1024, 128), F32)],
        compiler_params=params(),
    )(product_mapping_matrix)
    heads, x0, mapping = lax.optimization_barrier((heads, x0, mapping))
    kv = heads[:, 32:176, :]
    own = heads[:, 160:176, 0:128]
    kva = lax.ppermute(kv, ("c", "x"), ACROSS)
    kvb = lax.ppermute(kv, ("c", "x"), ACROSS_NEXT)
    swapped = lax.ppermute(own, "x", SWAP)
    x1 = lax.ppermute(x0, "x", SWAP)
    below, above = [heads[:, 0:32, :]], [heads[:, 0:32, :]]
    for step in range(4):
        below.append(lax.ppermute(below[-1], "z", UP))
        if step < 3:
            above.append(lax.ppermute(above[-1], "z", DOWN))
        if step == 1:
            below[2], swapped = lax.optimization_barrier((below[2], swapped))


    state = pl.pallas_call(
        attend_kernel,
        in_specs=[ARRAY] * 9,
        out_specs=ARRAY,
        out_shape=jax.ShapeDtypeStruct((2, 3, 128, 128), F32),
        scratch_shapes=[pltpu.VMEM((2, 128, 5 * 256), F32)],
        compiler_params=params(),
    )(own, swapped, kva, kvb, below[0], below[1], above[1], below[2], above[2])
    parts = pl.pallas_call(
        finish_kernel,
        in_specs=[ARRAY] * 10,
        out_specs=ARRAY,
        out_shape=jax.ShapeDtypeStruct((8, 2, 48, 256), BF16),
        scratch_shapes=[pltpu.VMEM((2, 128, 3 * 256), F32)],
        compiler_params=params(),
    )(own, swapped, kva, kvb, below[3], above[3], below[4], state, x0, x1)

    parts = lax.all_to_all(parts.reshape(16, 48, 256), ("q", "x"), 0, 0, tiled=True)

    fresh, sides = pl.pallas_call(
        refresh_kernel,
        in_specs=[SCALARS] + [ARRAY] * 8,
        out_specs=[ARRAY] * 2,
        out_shape=[jax.ShapeDtypeStruct((64, 256), BF16), jax.ShapeDtypeStruct((32, 128), BF16)],
        compiler_params=params(),
    )(sequence_valid_flags, parts, gate, prior, flags, attend_final_matrix, g2, first, other)

    sides = gather(sides, ("z", "x"), 16)
    band = lax.ppermute(sides[:, 16:32, :], ALL, MIRROR)
    parts, sides = lax.optimization_barrier((parts, sides))
    theirs = lax.ppermute(parts[:, 16:48, :], "c", SWAP)
    factors = pl.pallas_call(
        pack_kernel,
        in_specs=[ARRAY] * 2,
        out_specs=ARRAY,
        out_shape=jax.ShapeDtypeStruct((256, 1024), BF16),
        scratch_shapes=[pltpu.VMEM((2, 1024, 128), F32)],
        cost_estimate=pl.CostEstimate(flops=0, bytes_accessed=4 << 20, transcendentals=0),
        compiler_params=params(),
    )(parts, theirs)
    mapped = pl.pallas_call(
        map_kernel,
        grid=(4,),
        in_specs=[whole((16, 32, 128)), whole((128, 4096))],
        out_specs=pl.BlockSpec((4, 1024, 256), lambda i: (i, 0, 0)),
        out_shape=jax.ShapeDtypeStruct((16, 1024, 256), BF16),
        scratch_shapes=[pltpu.VMEM((256, 128), F32)],
        cost_estimate=pl.CostEstimate(flops=4 << 30, bytes_accessed=20 << 20, transcendentals=0),
        compiler_params=params(),
    )(sides, mapping)
    pair_out = pl.pallas_call(
        outer_kernel,
        in_specs=[SCALARS] * 2 + [ARRAY] * 4,
        out_specs=pl.BlockSpec(memory_space=pl.ANY),
        out_shape=jax.ShapeDtypeStruct((32, 256, 128), BF16),
        scratch_shapes=[
            pltpu.VMEM((8, 256, 128), F32),
            pltpu.VMEM((1024, 128), F32),
            pltpu.VMEM((256, 1024), BF16),
            pltpu.VMEM((32, 256, 128), BF16),
            pltpu.SemaphoreType.DMA((8,)),
        ],
        compiler_params=params(),
    )(sequence_valid_flags, position_valid_flags, factors, band, mapped, couple_activity)
    return fresh.reshape(2, 32, 256), pair_out


def solution(mesh):
    mesh = Mesh(mesh.devices.reshape(8, 2, 8, 2), ALL)
    wide, narrow = ("q", "c"), ("z", "x")
    in_specs = (P(narrow, wide, None), P(wide, narrow, None), P(), P(wide)) + (P(),) * 12
    out_specs = (P(narrow, wide, None), P(wide, narrow, None))
    return jax.shard_map(local, mesh=mesh, in_specs=in_specs, out_specs=out_specs, check_vma=False)
```

```python
import jax
import jax.numpy as jnp
from jax import lax
from jax.experimental import pallas as pl
from jax.experimental.pallas import tpu as pltpu
from jax.sharding import Mesh, PartitionSpec as P

EPS = 1e-05
BIG = 1000000000.0
F32 = jnp.float32
BF16 = jnp.bfloat16
VMEM = 40 * 1024 * 1024
FULL = 60 * 1024 * 1024
ALL = ("q", "c", "z", "x")


def dot(a, b, dims):
    return lax.dot_general(a, b, (dims, ((), ())), preferred_element_type=F32)


NN = ((1,), (0,))
NT = ((1,), (1,))
TN = ((0,), (0,))
TT = ((0,), (1,))


def center_and_scale(values):
    center = values - jnp.mean(values, axis=-1, keepdims=True)
    spread = jnp.mean(center * center, axis=-1, keepdims=True)
    return center * lax.rsqrt(spread + EPS)


def row_of(flags, count):
    lane = lax.broadcasted_iota(jnp.int32, (count, 256), 1)
    row = lax.broadcasted_iota(jnp.int32, (count, 256), 0)
    return jnp.sum(jnp.where(lane == row * 8, flags, 0.0), axis=1, keepdims=True)


def front_kernel(
    live_ref,
    pair_ref,
    seq_ref,
    flags_ref,
    g1_ref,
    ask_ref,
    look_ref,
    cont_ref,
    sig_ref,
    gp_ref,
    head_ref,
    g2_ref,
    other_ref,
    msg_ref,
    gate_ref,
    prior_ref,
    right_ref,
    bias_scr,
    norm_scr,
):
    step = pl.program_id(0)
    rows = pair_ref.shape[0]
    first_row = (lax.axis_index("z") * 2 + lax.axis_index("x")) * 2

    pair = pair_ref[...].reshape(rows * 256, 128).astype(F32)
    pair = (center_and_scale(pair) * gp_ref[...]).astype(BF16)
    bias = dot(head_ref[...], pair, NT)
    for r in range(rows):
        for i in range(2):
            bias_scr[i, pl.ds(pl.multiple_of((step * rows + r) * 8, 8), 8), :] = bias[
                :, r * 256 + i * 128 : r * 256 + i * 128 + 128
            ]

    @pl.when(step == 0)
    def _():
        raw = seq_ref[...].astype(F32)
        base = center_and_scale(raw)
        normed = (base * g1_ref[...]).astype(BF16)
        keys = dot(look_ref[...], normed, TT).astype(BF16)
        values = dot(cont_ref[...], normed, TT).astype(BF16)
        for h in range(8):
            for s in range(2):
                cut = (slice(h * 32, h * 32 + 32), slice(s * 256, s * 256 + 256))
                msg_ref[h, 32 + s * 32 : 64 + s * 32, :] = keys[cut]
                msg_ref[h, 96 + s * 32 : 128 + s * 32, :] = values[cut]
        wide = normed.astype(F32)
        for i in range(2):
            norm_scr[i] = wide[:, i * 128 : (i + 1) * 128]
            norm_scr[2 + i] = raw[:, i * 128 : (i + 1) * 128]
        cuts = [norm_scr[i, pl.ds(0, 64, stride=8), :] for i in range(4)]
        band = jnp.concatenate(cuts[:2], axis=1).astype(BF16)
        prior_ref[...] = jnp.concatenate(cuts[2:], axis=1)
        gate_ref[...] = jax.nn.sigmoid(dot(band, sig_ref[...], NN))
        query = (dot(band, ask_ref[...], NN) * 32 ** (-0.5)).astype(BF16).astype(F32)
        flags = flags_ref[...].astype(F32)
        row = lax.broadcasted_iota(jnp.int32, (16, 128), 0)
        mask = jnp.where(row == 0, flags[0:1], jnp.where(row == 1, flags[1:2], 0.0))
        for h in range(8):
            parts = [
                query[s * 32 + g * 16 : s * 32 + g * 16 + 16, h * 32 : h * 32 + 32]
                for g in range(2)
                for s in range(2)
            ]
            msg_ref[h, 160:176, :] = jnp.concatenate(parts + [mask], axis=1).astype(BF16)
        again = (base * g2_ref[...]).astype(BF16)
        right = dot(other_ref[...], again, NT)
        flags = jnp.concatenate([flags[0:1], flags[1:2]], axis=1)
        for s in range(2):
            live = live_ref[first_row + s].astype(F32) * flags
            right_ref[s] = (right[:, s * 256 : (s + 1) * 256] * live).astype(BF16)

    @pl.when(step == pl.num_programs(0) - 1)
    def _():
        for h in range(8):
            for i in range(2):
                msg_ref[h, 0:32, i * 128 : i * 128 + 128] = bias_scr[
                    i, pl.ds(h, 32, stride=8), :
                ].astype(BF16)


def split3(value):
    high = value.astype(BF16).astype(F32)
    rest = value - high
    middle = rest.astype(BF16).astype(F32)
    return high, middle, rest - middle


def attend_blocks(own_ref, swapped_ref, kva_ref, kvb_ref, blocks, extra_scr):
    c, x, z = lax.axis_index("c"), lax.axis_index("x"), lax.axis_index("z")
    places = [lax.rem(z + offset * (1 - 2 * c) + 8, 8) for offset, _ in blocks]
    block = lax.broadcasted_iota(jnp.int32, (128, 128), 1) // 32
    for k, (place, (_, bias_ref)) in enumerate(zip(places, blocks)):
        mask = jnp.concatenate(
            [kva_ref[place, 128 + i : 129 + i, 128:256].astype(F32) for i in range(2)], axis=1
        )
        for g in range(2):
            piece = bias_ref[:, g * 16 : g * 16 + 16, :].reshape(128, 256).astype(F32)
            extra_scr[g, :, k * 256 : (k + 1) * 256] = piece + BIG * (mask - 1.0)
    own = own_ref[...].reshape(128, 128)
    swapped = swapped_ref[...].reshape(128, 128)
    states = []
    for a, kv_ref in enumerate((kva_ref, kvb_ref)):
        query = jnp.where((c ^ a) == x, own, swapped).astype(F32)
        keys = jnp.concatenate([kv_ref[place, 0:64, :] for place in places], axis=1)
        values = jnp.concatenate([kv_ref[place, 64:128, :] for place in places], axis=1)
        keys = jnp.concatenate([keys, keys], axis=0)
        values = jnp.concatenate([values, values], axis=0)
        state = [jnp.zeros((128, 128), F32)] * 3
        for g in range(2):
            for s in range(2):
                here = block == g * 2 + s
                picked = jnp.where(here, query, 0.0).astype(BF16)
                scores = dot(picked, keys, NN) + extra_scr[g]
                top = jnp.max(scores, axis=1, keepdims=True)
                expo = jnp.exp(scores - top)
                total = jnp.sum(expo, axis=1, keepdims=True)
                mixed = dot(expo.astype(BF16), values, NT)
                state = [jnp.where(here, new, old) for new, old in zip((mixed, top, total), state)]
        states.append(state)
    return states


def attend_kernel(own_ref, swapped_ref, kva_ref, kvb_ref, *refs):
    *bias_refs, out_ref, extra_scr = refs
    blocks = list(zip((0, -1, 1, -2, 2, -3, 3), bias_refs))
    states = attend_blocks(own_ref, swapped_ref, kva_ref, kvb_ref, blocks, extra_scr)
    for a in range(2):
        for i in range(3):
            out_ref[a, i] = states[a][i]


def finish_kernel(own_ref, swapped_ref, kva_ref, kvb_ref, *refs):
    *bias_refs, state_ref, x0_ref, x1_ref, out_ref, extra_scr = refs
    c, x = lax.axis_index("c"), lax.axis_index("x")
    for q in range(8):
        out_ref[q, x, 16:48, :] = x0_ref[x]
        out_ref[q, 1 - x, 16:48, :] = x1_ref[x]
    inner = lax.broadcasted_iota(jnp.int32, (128, 128), 1) % 32
    blocks = list(zip((-4,), bias_refs))
    states = attend_blocks(own_ref, swapped_ref, kva_ref, kvb_ref, blocks, extra_scr)
    for a in range(2):
        mixed, top, total = states[a]
        other_mixed, other_top, other_total = (state_ref[a, i] for i in range(3))
        best = jnp.maximum(top, other_top)
        weight, other_weight = jnp.exp(top - best), jnp.exp(other_top - best)
        total = total * weight + other_total * other_weight
        mixed = (mixed * weight + other_mixed * other_weight) / total
        stats = jnp.zeros((128, 128), F32)
        for t, piece in enumerate(split3(best) + split3(total)):
            stats = jnp.where(inner == t, piece, stats)
        joined = jnp.concatenate([mixed, stats], axis=1).astype(BF16)
        for q in range(8):
            out_ref[q, c ^ a, 0:16, :] = joined[q * 16 : q * 16 + 16]


def refresh_kernel(
    live_ref,
    parts_ref,
    gate_ref,
    prior_ref,
    flags_ref,
    final_ref,
    g2_ref,
    first_ref,
    other_ref,
    fresh_ref,
    sides_ref,
):
    first_row = (lax.axis_index("z") * 2 + lax.axis_index("x")) * 2
    flags = flags_ref[...].astype(F32)
    band = row_of(jnp.concatenate([flags[0:1], flags[1:2]], axis=1), 32)
    live = jnp.concatenate([band * live_ref[first_row + s].astype(F32) for s in range(2)], axis=0)
    rows = lax.broadcasted_iota(jnp.int32, (128, 128), 0)
    lanes = lax.broadcasted_iota(jnp.int32, (128, 128), 1)
    spread = [jnp.where(rows == (lanes // 32) * 32 + t, 1.0, 0.0).astype(BF16) for t in range(6)]
    tops, totals, mixes = [], [], []
    for x in range(2):
        mixes.append(
            jnp.concatenate([parts_ref[2 * h + x, 0:16, 0:128] for h in range(8)], axis=0).astype(F32)
        )
        stats = jnp.concatenate([parts_ref[2 * h + x, 0:16, 128:256] for h in range(8)], axis=0)
        wide = [dot(stats, spread[t], NN) for t in range(6)]
        tops.append(wide[0] + wide[1] + wide[2])
        totals.append(wide[3] + wide[4] + wide[5])
    top = jnp.maximum(tops[0], tops[1])
    weights = [totals[i] * jnp.exp(tops[i] - top) for i in range(2)]
    attended = (weights[0] * mixes[0] + weights[1] * mixes[1]) / (weights[0] + weights[1])
    lined = []
    for s in range(2):
        for g in range(2):
            cut = (g * 2 + s) * 32
            lined.append(
                jnp.concatenate(
                    [attended[h * 16 : h * 16 + 16, cut : cut + 32] for h in range(8)], axis=1
                )
            )
    attended = jnp.concatenate(lined, axis=0)
    gated = (gate_ref[...] * attended).astype(BF16)
    fresh = (prior_ref[...] + dot(gated, final_ref[...], NN)).astype(BF16)
    fresh_ref[...] = fresh
    again = (center_and_scale(fresh.astype(F32)) * g2_ref[...]).astype(BF16)
    for i, factor in enumerate((first_ref, other_ref)):
        side = dot(again, factor[...], NT) * live
        parts = [side[s * 32 + g * 16 : s * 32 + g * 16 + 16] for g in range(2) for s in range(2)]
        sides_ref[i * 16 : i * 16 + 16, :] = jnp.concatenate(parts, axis=1).astype(BF16)


def pack_kernel(mine_ref, theirs_ref, factors_ref, factor_scr):
    swapped = lax.axis_index("c") == 1
    turn = lax.axis_index("z") * 2 + lax.axis_index("x")
    for q in range(8):
        for c in range(2):
            for x in range(2):
                mine = mine_ref[2 * q + x, 16:48, :].astype(F32)
                theirs = theirs_ref[2 * q + x].astype(F32)
                piece = jnp.where(swapped == (c == 1), mine, theirs)
                place = pl.multiple_of((x * 16 + (turn ^ (2 * q + c))) * 32, 32)
                for i in range(2):
                    factor_scr[i, pl.ds(place, 32), :] = piece[:, i * 128 : i * 128 + 128]
    for k in range(8):
        rows = []
        for d in range(k * 4, k * 4 + 4):
            rows.append(
                jnp.concatenate([factor_scr[i, pl.ds(d, 32, stride=32), :] for i in range(2)], axis=1)
            )
        factors_ref[:, k * 128 : (k + 1) * 128] = jnp.concatenate(rows, axis=0).T.astype(BF16)


def line_kernel(map_ref, mapping_ref, scr):
    scr[...] = map_ref[...].astype(F32)
    for d in range(32):
        piece = scr[pl.ds(d, 32, stride=32), :].astype(BF16)
        for k in range(4):
            mapping_ref[k * 32 : k * 32 + 32, d * 128 : (d + 1) * 128] = piece


def map_kernel(sides_ref, mapping_ref, out_ref, side_scr):
    step = pl.program_id(0)

    @pl.when(step == 0)
    def _():
        for n in range(16):
            side_scr[n * 16 : n * 16 + 16, :] = sides_ref[n, 0:16, :].astype(F32)

    block = lax.broadcasted_iota(jnp.int32, (16, 128), 1) // 32
    group = step // 2
    lefts = []
    for r in range(8):
        lined = side_scr[pl.ds((step % 2) * 8 + r, 16, stride=16), :]
        for s in range(2):
            lefts.append(jnp.where(block == group * 2 + s, lined, 0.0))
    left = jnp.concatenate(lefts, axis=0).astype(BF16)
    for d in range(0, 32, 2):
        mapped = dot(left, mapping_ref[:, d * 128 : (d + 2) * 128], NN).astype(BF16)
        for e in range(2):
            for r in range(8):
                out_ref[r // 2, (d + e) * 32 : (d + e) * 32 + 32, (r % 2) * 128 : (r % 2) * 128 + 128] = (
                    mapped[r * 32 : r * 32 + 32, e * 128 : e * 128 + 128]
                )


def outer_kernel(
    live_ref,
    flags_ref,
    factors_ref,
    band_ref,
    mapped_ref,
    pair_ref,
    out_ref,
    band_scr,
    full_scr,
    done_scr,
    sems,
):
    turned = jnp.concatenate([band_ref[n].astype(F32) for n in range(16)], axis=0).T
    empty = jnp.zeros((32, 96), F32)
    for s in range(2):
        for n in range(16):
            parts = [
                turned[g * 64 + s * 32 : g * 64 + s * 32 + 32, n * 16 : n * 16 + 16] for g in range(2)
            ]
            band_scr[pl.ds(s * 16 + n, 32, stride=32), :] = jnp.concatenate(parts + [empty], axis=1)
    slot = lax.broadcasted_iota(jnp.int32, (256, 128), 0) % 8
    for i in range(8):
        band = band_scr[i * 128 : (i + 1) * 128, :].T[0:32]
        band = jnp.broadcast_to(band[:, None, :], (32, 8, 128)).reshape(256, 128)
        piece = factors_ref[:, i * 128 : (i + 1) * 128].astype(F32)
        full_scr[:, i * 128 : (i + 1) * 128] = jnp.where(slot == 0, band, piece).astype(BF16)

    nvalid = jnp.int32(0)
    for s in range(32):
        nvalid += live_ref[s]
    copies = []
    for k in range(8):
        for r in range(k * 4, k * 4 + 4, 2):
            projected = dot(full_scr[...], mapped_ref[r // 2], NN)
            for i in range(2):
                scale = 1.0 / jnp.maximum((nvalid * flags_ref[(r + i) * 8]).astype(F32), 1.0)
                done_scr[r + i] = (
                    pair_ref[r + i].astype(F32) + projected[:, i * 128 : (i + 1) * 128] * scale
                ).astype(BF16)
        part = pl.ds(k * 4, 4)
        copies.append(pltpu.make_async_copy(done_scr.at[part], out_ref.at[part], sems.at[k]))
        copies[-1].start()
    for copy in copies:
        copy.wait()


def gather(value, axes, count):
    tiled = jnp.broadcast_to(value[None], (count,) + value.shape)
    return lax.all_to_all(tiled, axes, 0, 0, tiled=True)


def whole(shape):
    return pl.BlockSpec(shape, lambda *_: (0,) * len(shape))


SCALARS = pl.BlockSpec(memory_space=pltpu.SMEM)
ARRAY = pl.BlockSpec(memory_space=pltpu.VMEM)


def params():
    return pltpu.CompilerParams(vmem_limit_bytes=VMEM)


MIRROR = [(w * 16 + n, (n ^ w) * 16 + w) for w in range(16) for n in range(16)]
ACROSS = [(a * 2 + b, b * 2 + a) for a in range(2) for b in range(2)]
ACROSS_NEXT = [(a * 2 + b, (1 - b) * 2 + a) for a in range(2) for b in range(2)]
SWAP = [(0, 1), (1, 0)]
AHEAD = [(c * 8 + i, c * 8 + (i + 1 - 2 * c) % 8) for c in range(2) for i in range(8)]
BEHIND = [(c * 8 + i, c * 8 + (i - 1 + 2 * c) % 8) for c in range(2) for i in range(8)]


def local(
    sequence_activity,
    couple_activity,
    sequence_valid_flags,
    position_valid_flags,
    attend_scale_vector,
    asking_matrix,
    lookup_matrix,
    content_matrix,
    sigmoid_matrix,
    attend_final_matrix,
    couple_scale_vector,
    headwise_additive_matrix,
    product_scale_vector,
    first_factor_matrix,
    other_factor_matrix,
    product_mapping_matrix,
):
    g2 = product_scale_vector.reshape(1, 256)
    flags = position_valid_flags.reshape(2, 128)
    first, other = first_factor_matrix.T, other_factor_matrix.T

    message, gate, prior, right = pl.pallas_call(
        front_kernel,
        grid=(2,),
        in_specs=[SCALARS, pl.BlockSpec((16, 256, 128), lambda i: (i, 0, 0))]
        + [
            whole(s)
            for s in (
                (512, 256),
                (2, 128),
                (1, 256),
                (256, 256),
                (256, 256),
                (256, 256),
                (256, 256),
                (1, 128),
                (8, 128),
                (1, 256),
                (32, 256),
            )
        ],
        out_specs=[whole((8, 176, 256)), whole((64, 256)), whole((64, 256)), whole((2, 32, 256))],
        out_shape=[
            jax.ShapeDtypeStruct((8, 176, 256), BF16),
            jax.ShapeDtypeStruct((64, 256), F32),
            jax.ShapeDtypeStruct((64, 256), F32),
            jax.ShapeDtypeStruct((2, 32, 256), BF16),
        ],
        scratch_shapes=[pltpu.VMEM((2, 256, 128), F32), pltpu.VMEM((4, 512, 128), F32)],
        compiler_params=pltpu.CompilerParams(vmem_limit_bytes=FULL),
    )(
        sequence_valid_flags,
        couple_activity,
        sequence_activity.reshape(512, 256),
        flags,
        attend_scale_vector.reshape(1, 256),
        asking_matrix,
        lookup_matrix,
        content_matrix,
        sigmoid_matrix,
        couple_scale_vector.reshape(1, 128),
        headwise_additive_matrix.T,
        g2,
        other,
    )

    heads = lax.all_to_all(message, "q", 0, 0, tiled=True)
    x0 = lax.ppermute(right, ALL, MIRROR)
    mapping = pl.pallas_call(
        line_kernel,
        in_specs=[ARRAY],
        out_specs=ARRAY,
        out_shape=jax.ShapeDtypeStruct((128, 4096), BF16),
        scratch_shapes=[pltpu.VMEM((1024, 128), F32)],
        compiler_params=params(),
    )(product_mapping_matrix)
    heads, x0, mapping = lax.optimization_barrier((heads, x0, mapping))
    kv = heads[:, 32:176, :]
    own = heads[:, 160:176, 0:128]
    kva = lax.ppermute(kv, ("c", "x"), ACROSS)
    kvb = lax.ppermute(kv, ("c", "x"), ACROSS_NEXT)
    swapped = lax.ppermute(own, "x", SWAP)
    x1 = lax.ppermute(x0, "x", SWAP)
    below, above = [heads[:, 0:32, :]], [heads[:, 0:32, :]]
    for step in range(4):
        below.append(lax.ppermute(below[-1], ("c", "z"), AHEAD))
        if step < 3:
            above.append(lax.ppermute(above[-1], ("c", "z"), BEHIND))
        if step == 1:
            below[2], swapped = lax.optimization_barrier((below[2], swapped))


    state = pl.pallas_call(
        attend_kernel,
        in_specs=[ARRAY] * 11,
        out_specs=ARRAY,
        out_shape=jax.ShapeDtypeStruct((2, 3, 128, 128), F32),
        scratch_shapes=[pltpu.VMEM((2, 128, 7 * 256), F32)],
        compiler_params=params(),
    )(own, swapped, kva, kvb, below[0], below[1], above[1], below[2], above[2], below[3], above[3])
    parts = pl.pallas_call(
        finish_kernel,
        in_specs=[ARRAY] * 8,
        out_specs=ARRAY,
        out_shape=jax.ShapeDtypeStruct((8, 2, 48, 256), BF16),
        scratch_shapes=[pltpu.VMEM((2, 128, 256), F32)],
        compiler_params=params(),
    )(own, swapped, kva, kvb, below[4], state, x0, x1)

    parts = lax.all_to_all(parts.reshape(16, 48, 256), ("q", "x"), 0, 0, tiled=True)

    fresh, sides = pl.pallas_call(
        refresh_kernel,
        in_specs=[SCALARS] + [ARRAY] * 8,
        out_specs=[ARRAY] * 2,
        out_shape=[jax.ShapeDtypeStruct((64, 256), BF16), jax.ShapeDtypeStruct((32, 128), BF16)],
        compiler_params=params(),
    )(sequence_valid_flags, parts, gate, prior, flags, attend_final_matrix, g2, first, other)

    sides = gather(sides, ("z", "x"), 16)
    band = lax.ppermute(sides[:, 16:32, :], ALL, MIRROR)
    parts, sides = lax.optimization_barrier((parts, sides))
    theirs = lax.ppermute(parts[:, 16:48, :], "c", SWAP)
    factors = pl.pallas_call(
        pack_kernel,
        in_specs=[ARRAY] * 2,
        out_specs=ARRAY,
        out_shape=jax.ShapeDtypeStruct((256, 1024), BF16),
        scratch_shapes=[pltpu.VMEM((2, 1024, 128), F32)],
        cost_estimate=pl.CostEstimate(flops=0, bytes_accessed=4 << 20, transcendentals=0),
        compiler_params=params(),
    )(parts, theirs)
    mapped = pl.pallas_call(
        map_kernel,
        grid=(4,),
        in_specs=[whole((16, 32, 128)), whole((128, 4096))],
        out_specs=pl.BlockSpec((4, 1024, 256), lambda i: (i, 0, 0)),
        out_shape=jax.ShapeDtypeStruct((16, 1024, 256), BF16),
        scratch_shapes=[pltpu.VMEM((256, 128), F32)],
        cost_estimate=pl.CostEstimate(flops=4 << 30, bytes_accessed=20 << 20, transcendentals=0),
        compiler_params=params(),
    )(sides, mapping)
    pair_out = pl.pallas_call(
        outer_kernel,
        in_specs=[SCALARS] * 2 + [ARRAY] * 4,
        out_specs=pl.BlockSpec(memory_space=pl.ANY),
        out_shape=jax.ShapeDtypeStruct((32, 256, 128), BF16),
        scratch_shapes=[
            pltpu.VMEM((1024, 128), F32),
            pltpu.VMEM((256, 1024), BF16),
            pltpu.VMEM((32, 256, 128), BF16),
            pltpu.SemaphoreType.DMA((8,)),
        ],
        compiler_params=params(),
    )(sequence_valid_flags, position_valid_flags, factors, band, mapped, couple_activity)
    return fresh.reshape(2, 32, 256), pair_out


def solution(mesh):
    mesh = Mesh(mesh.devices.reshape(8, 2, 8, 2), ALL)
    wide, narrow = ("q", "c"), ("z", "x")
    in_specs = (P(narrow, wide, None), P(wide, narrow, None), P(), P(wide)) + (P(),) * 12
    out_specs = (P(narrow, wide, None), P(wide, narrow, None))
    return jax.shard_map(local, mesh=mesh, in_specs=in_specs, out_specs=out_specs, check_vma=False)
```

```python
import jax
import jax.numpy as jnp
from jax import lax
from jax.experimental import pallas as pl
from jax.experimental.pallas import tpu as pltpu
from jax.sharding import Mesh, PartitionSpec as P

EPS = 1e-05
BIG = 1000000000.0
F32 = jnp.float32
BF16 = jnp.bfloat16
VMEM = 40 * 1024 * 1024
FULL = 60 * 1024 * 1024
ALL = ("q", "c", "z", "x")


def dot(a, b, dims):
    return lax.dot_general(a, b, (dims, ((), ())), preferred_element_type=F32)


NN = ((1,), (0,))
NT = ((1,), (1,))
TN = ((0,), (0,))
TT = ((0,), (1,))


def center_and_scale(values):
    center = values - jnp.mean(values, axis=-1, keepdims=True)
    spread = jnp.mean(center * center, axis=-1, keepdims=True)
    return center * lax.rsqrt(spread + EPS)


def row_of(flags, count):
    lane = lax.broadcasted_iota(jnp.int32, (count, 256), 1)
    row = lax.broadcasted_iota(jnp.int32, (count, 256), 0)
    return jnp.sum(jnp.where(lane == row * 8, flags, 0.0), axis=1, keepdims=True)


def front_kernel(
    live_ref,
    pair_ref,
    seq_ref,
    flags_ref,
    g1_ref,
    ask_ref,
    look_ref,
    cont_ref,
    sig_ref,
    gp_ref,
    head_ref,
    g2_ref,
    other_ref,
    msg_ref,
    gate_ref,
    prior_ref,
    right_ref,
    bias_scr,
    norm_scr,
):
    step = pl.program_id(0)
    rows = pair_ref.shape[0]
    first_row = (lax.axis_index("z") * 2 + lax.axis_index("x")) * 2

    pair = pair_ref[...].reshape(rows * 256, 128).astype(F32)
    pair = (center_and_scale(pair) * gp_ref[...]).astype(BF16)
    bias = dot(head_ref[...], pair, NT)
    for r in range(rows):
        for i in range(2):
            bias_scr[i, pl.ds(pl.multiple_of((step * rows + r) * 8, 8), 8), :] = bias[
                :, r * 256 + i * 128 : r * 256 + i * 128 + 128
            ]

    @pl.when(step == 0)
    def _():
        raw = seq_ref[...].astype(F32)
        base = center_and_scale(raw)
        normed = (base * g1_ref[...]).astype(BF16)
        keys = dot(look_ref[...], normed, TT).astype(BF16)
        values = dot(cont_ref[...], normed, TT).astype(BF16)
        for h in range(8):
            for s in range(2):
                cut = (slice(h * 32, h * 32 + 32), slice(s * 256, s * 256 + 256))
                msg_ref[h, 32 + s * 32 : 64 + s * 32, :] = keys[cut]
                msg_ref[h, 96 + s * 32 : 128 + s * 32, :] = values[cut]
        wide = normed.astype(F32)
        for i in range(2):
            norm_scr[i] = wide[:, i * 128 : (i + 1) * 128]
            norm_scr[2 + i] = raw[:, i * 128 : (i + 1) * 128]
        cuts = [norm_scr[i, pl.ds(0, 64, stride=8), :] for i in range(4)]
        band = jnp.concatenate(cuts[:2], axis=1).astype(BF16)
        prior_ref[...] = jnp.concatenate(cuts[2:], axis=1)
        gate_ref[...] = jax.nn.sigmoid(dot(band, sig_ref[...], NN))
        query = (dot(band, ask_ref[...], NN) * 32 ** (-0.5)).astype(BF16).astype(F32)
        flags = flags_ref[...].astype(F32)
        row = lax.broadcasted_iota(jnp.int32, (16, 128), 0)
        mask = jnp.where(row == 0, flags[0:1], jnp.where(row == 1, flags[1:2], 0.0))
        for h in range(8):
            parts = [
                query[s * 32 + g * 16 : s * 32 + g * 16 + 16, h * 32 : h * 32 + 32]
                for g in range(2)
                for s in range(2)
            ]
            msg_ref[h, 160:176, :] = jnp.concatenate(parts + [mask], axis=1).astype(BF16)
        again = (base * g2_ref[...]).astype(BF16)
        right = dot(other_ref[...], again, NT)
        flags = jnp.concatenate([flags[0:1], flags[1:2]], axis=1)
        for s in range(2):
            live = live_ref[first_row + s].astype(F32) * flags
            right_ref[s] = (right[:, s * 256 : (s + 1) * 256] * live).astype(BF16)

    @pl.when(step == pl.num_programs(0) - 1)
    def _():
        for h in range(8):
            for i in range(2):
                msg_ref[h, 0:32, i * 128 : i * 128 + 128] = bias_scr[
                    i, pl.ds(h, 32, stride=8), :
                ].astype(BF16)


def split3(value):
    high = value.astype(BF16).astype(F32)
    rest = value - high
    middle = rest.astype(BF16).astype(F32)
    return high, middle, rest - middle


def attend_blocks(own_ref, swapped_ref, kva_ref, kvb_ref, blocks, extra_scr):
    c, x, z = lax.axis_index("c"), lax.axis_index("x"), lax.axis_index("z")
    places = [lax.rem(z + offset * (1 - 2 * c) + 8, 8) for offset, _ in blocks]
    block = lax.broadcasted_iota(jnp.int32, (128, 128), 1) // 32
    for k, (place, (_, bias_ref)) in enumerate(zip(places, blocks)):
        mask = jnp.concatenate(
            [kva_ref[place, 128 + i : 129 + i, 128:256].astype(F32) for i in range(2)], axis=1
        )
        for g in range(2):
            piece = bias_ref[:, g * 16 : g * 16 + 16, :].reshape(128, 256).astype(F32)
            extra_scr[g, :, k * 256 : (k + 1) * 256] = piece + BIG * (mask - 1.0)
    own = own_ref[...].reshape(128, 128)
    swapped = swapped_ref[...].reshape(128, 128)
    states = []
    for a, kv_ref in enumerate((kva_ref, kvb_ref)):
        query = jnp.where((c ^ a) == x, own, swapped).astype(F32)
        keys = jnp.concatenate([kv_ref[place, 0:64, :] for place in places], axis=1)
        values = jnp.concatenate([kv_ref[place, 64:128, :] for place in places], axis=1)
        keys = jnp.concatenate([keys, keys], axis=0)
        values = jnp.concatenate([values, values], axis=0)
        state = [jnp.zeros((128, 128), F32)] * 3
        for g in range(2):
            for s in range(2):
                here = block == g * 2 + s
                picked = jnp.where(here, query, 0.0).astype(BF16)
                scores = dot(picked, keys, NN) + extra_scr[g]
                top = jnp.max(scores, axis=1, keepdims=True)
                expo = jnp.exp(scores - top)
                total = jnp.sum(expo, axis=1, keepdims=True)
                mixed = dot(expo.astype(BF16), values, NT)
                state = [jnp.where(here, new, old) for new, old in zip((mixed, top, total), state)]
        states.append(state)
    return states


def attend_kernel(own_ref, swapped_ref, kva_ref, kvb_ref, *refs):
    *bias_refs, out_ref, extra_scr = refs
    blocks = list(zip((0, -1, 1, -2, 2, -3, 3), bias_refs))
    states = attend_blocks(own_ref, swapped_ref, kva_ref, kvb_ref, blocks, extra_scr)
    for a in range(2):
        for i in range(3):
            out_ref[a, i] = states[a][i]


def finish_kernel(own_ref, swapped_ref, kva_ref, kvb_ref, *refs):
    *bias_refs, state_ref, x0_ref, x1_ref, out_ref, extra_scr = refs
    c, x = lax.axis_index("c"), lax.axis_index("x")
    for q in range(8):
        out_ref[q, x, 16:48, :] = x0_ref[x]
        out_ref[q, 1 - x, 16:48, :] = x1_ref[x]
    inner = lax.broadcasted_iota(jnp.int32, (128, 128), 1) % 32
    blocks = list(zip((-4,), bias_refs))
    states = attend_blocks(own_ref, swapped_ref, kva_ref, kvb_ref, blocks, extra_scr)
    for a in range(2):
        mixed, top, total = states[a]
        other_mixed, other_top, other_total = (state_ref[a, i] for i in range(3))
        best = jnp.maximum(top, other_top)
        weight, other_weight = jnp.exp(top - best), jnp.exp(other_top - best)
        total = total * weight + other_total * other_weight
        mixed = (mixed * weight + other_mixed * other_weight) / total
        stats = jnp.zeros((128, 128), F32)
        for t, piece in enumerate(split3(best) + split3(total)):
            stats = jnp.where(inner == t, piece, stats)
        joined = jnp.concatenate([mixed, stats], axis=1).astype(BF16)
        for q in range(8):
            out_ref[q, c ^ a, 0:16, :] = joined[q * 16 : q * 16 + 16]


def refresh_kernel(
    live_ref,
    parts_ref,
    gate_ref,
    prior_ref,
    flags_ref,
    final_ref,
    g2_ref,
    first_ref,
    other_ref,
    fresh_ref,
    sides_ref,
):
    first_row = (lax.axis_index("z") * 2 + lax.axis_index("x")) * 2
    flags = flags_ref[...].astype(F32)
    band = row_of(jnp.concatenate([flags[0:1], flags[1:2]], axis=1), 32)
    live = jnp.concatenate([band * live_ref[first_row + s].astype(F32) for s in range(2)], axis=0)
    rows = lax.broadcasted_iota(jnp.int32, (128, 128), 0)
    lanes = lax.broadcasted_iota(jnp.int32, (128, 128), 1)
    spread = jnp.concatenate(
        [jnp.where(rows == (lanes // 32) * 32 + t, 1.0, 0.0).astype(BF16) for t in range(6)], axis=1
    )
    tops, totals, mixes = [], [], []
    for x in range(2):
        mixes.append(
            jnp.concatenate([parts_ref[2 * h + x, 0:16, 0:128] for h in range(8)], axis=0).astype(F32)
        )
        stats = jnp.concatenate([parts_ref[2 * h + x, 0:16, 128:256] for h in range(8)], axis=0)
        wide = dot(stats, spread, NN)
        wide = [wide[:, t * 128 : (t + 1) * 128] for t in range(6)]
        tops.append(wide[0] + wide[1] + wide[2])
        totals.append(wide[3] + wide[4] + wide[5])
    top = jnp.maximum(tops[0], tops[1])
    weights = [totals[i] * jnp.exp(tops[i] - top) for i in range(2)]
    attended = (weights[0] * mixes[0] + weights[1] * mixes[1]) / (weights[0] + weights[1])
    lined = []
    for s in range(2):
        for g in range(2):
            cut = (g * 2 + s) * 32
            lined.append(
                jnp.concatenate(
                    [attended[h * 16 : h * 16 + 16, cut : cut + 32] for h in range(8)], axis=1
                )
            )
    attended = jnp.concatenate(lined, axis=0)
    gated = (gate_ref[...] * attended).astype(BF16)
    fresh = (prior_ref[...] + dot(gated, final_ref[...], NN)).astype(BF16)
    fresh_ref[...] = fresh
    again = (center_and_scale(fresh.astype(F32)) * g2_ref[...]).astype(BF16)
    for i, factor in enumerate((first_ref, other_ref)):
        side = dot(again, factor[...], NT) * live
        parts = [side[s * 32 + g * 16 : s * 32 + g * 16 + 16] for g in range(2) for s in range(2)]
        sides_ref[i * 16 : i * 16 + 16, :] = jnp.concatenate(parts, axis=1).astype(BF16)


def pack_kernel(mine_ref, theirs_ref, factors_ref, factor_scr):
    swapped = lax.axis_index("c") == 1
    turn = lax.axis_index("z") * 2 + lax.axis_index("x")
    for q in range(8):
        for c in range(2):
            for x in range(2):
                mine = mine_ref[2 * q + x, 16:48, :].astype(F32)
                theirs = theirs_ref[2 * q + x].astype(F32)
                piece = jnp.where(swapped == (c == 1), mine, theirs)
                place = pl.multiple_of((x * 16 + (turn ^ (2 * q + c))) * 32, 32)
                for i in range(2):
                    factor_scr[i, pl.ds(place, 32), :] = piece[:, i * 128 : i * 128 + 128]
    for k in range(8):
        rows = []
        for d in range(k * 4, k * 4 + 4):
            rows.append(
                jnp.concatenate([factor_scr[i, pl.ds(d, 32, stride=32), :] for i in range(2)], axis=1)
            )
        factors_ref[:, k * 128 : (k + 1) * 128] = jnp.concatenate(rows, axis=0).T.astype(BF16)


def line_kernel(map_ref, mapping_ref, scr):
    scr[...] = map_ref[...].astype(F32)
    for d in range(32):
        piece = scr[pl.ds(d, 32, stride=32), :].astype(BF16)
        for k in range(4):
            mapping_ref[k * 32 : k * 32 + 32, d * 128 : (d + 1) * 128] = piece


def map_kernel(sides_ref, mapping_ref, out_ref, side_scr):
    step = pl.program_id(0)

    @pl.when(step == 0)
    def _():
        for n in range(16):
            side_scr[n * 16 : n * 16 + 16, :] = sides_ref[n, 0:16, :].astype(F32)

    block = lax.broadcasted_iota(jnp.int32, (16, 128), 1) // 32
    group = step // 2
    lefts = []
    for r in range(8):
        lined = side_scr[pl.ds((step % 2) * 8 + r, 16, stride=16), :]
        for s in range(2):
            lefts.append(jnp.where(block == group * 2 + s, lined, 0.0))
    left = jnp.concatenate(lefts, axis=0).astype(BF16)
    for d in range(0, 32, 2):
        mapped = dot(left, mapping_ref[:, d * 128 : (d + 2) * 128], NN).astype(BF16)
        for e in range(2):
            for r in range(8):
                out_ref[r // 2, (d + e) * 32 : (d + e) * 32 + 32, (r % 2) * 128 : (r % 2) * 128 + 128] = (
                    mapped[r * 32 : r * 32 + 32, e * 128 : e * 128 + 128]
                )


def outer_kernel(
    live_ref,
    flags_ref,
    factors_ref,
    band_ref,
    mapped_ref,
    pair_ref,
    out_ref,
    band_scr,
    full_scr,
    done_scr,
    sems,
):
    turned = jnp.concatenate([band_ref[n].astype(F32) for n in range(16)], axis=0).T
    empty = jnp.zeros((32, 96), F32)
    for s in range(2):
        for n in range(16):
            parts = [
                turned[g * 64 + s * 32 : g * 64 + s * 32 + 32, n * 16 : n * 16 + 16] for g in range(2)
            ]
            band_scr[pl.ds(s * 16 + n, 32, stride=32), :] = jnp.concatenate(parts + [empty], axis=1)
    slot = lax.broadcasted_iota(jnp.int32, (256, 128), 0) % 8
    for i in range(8):
        band = band_scr[i * 128 : (i + 1) * 128, :].T[0:32]
        band = jnp.broadcast_to(band[:, None, :], (32, 8, 128)).reshape(256, 128)
        piece = factors_ref[:, i * 128 : (i + 1) * 128].astype(F32)
        full_scr[:, i * 128 : (i + 1) * 128] = jnp.where(slot == 0, band, piece).astype(BF16)

    nvalid = jnp.int32(0)
    for s in range(32):
        nvalid += live_ref[s]
    copies = []
    for k in range(8):
        for r in range(k * 4, k * 4 + 4, 2):
            projected = dot(full_scr[...], mapped_ref[r // 2], NN)
            for i in range(2):
                scale = 1.0 / jnp.maximum((nvalid * flags_ref[(r + i) * 8]).astype(F32), 1.0)
                done_scr[r + i] = (
                    pair_ref[r + i].astype(F32) + projected[:, i * 128 : (i + 1) * 128] * scale
                ).astype(BF16)
        part = pl.ds(k * 4, 4)
        copies.append(pltpu.make_async_copy(done_scr.at[part], out_ref.at[part], sems.at[k]))
        copies[-1].start()
    for copy in copies:
        copy.wait()


def gather(value, axes, count):
    tiled = jnp.broadcast_to(value[None], (count,) + value.shape)
    return lax.all_to_all(tiled, axes, 0, 0, tiled=True)


def whole(shape):
    return pl.BlockSpec(shape, lambda *_: (0,) * len(shape))


SCALARS = pl.BlockSpec(memory_space=pltpu.SMEM)
ARRAY = pl.BlockSpec(memory_space=pltpu.VMEM)


def params():
    return pltpu.CompilerParams(vmem_limit_bytes=VMEM)


MIRROR = [(w * 16 + n, (n ^ w) * 16 + w) for w in range(16) for n in range(16)]
ACROSS = [(a * 2 + b, b * 2 + a) for a in range(2) for b in range(2)]
ACROSS_NEXT = [(a * 2 + b, (1 - b) * 2 + a) for a in range(2) for b in range(2)]
SWAP = [(0, 1), (1, 0)]
AHEAD = [(c * 8 + i, c * 8 + (i + 1 - 2 * c) % 8) for c in range(2) for i in range(8)]
BEHIND = [(c * 8 + i, c * 8 + (i - 1 + 2 * c) % 8) for c in range(2) for i in range(8)]


def local(
    sequence_activity,
    couple_activity,
    sequence_valid_flags,
    position_valid_flags,
    attend_scale_vector,
    asking_matrix,
    lookup_matrix,
    content_matrix,
    sigmoid_matrix,
    attend_final_matrix,
    couple_scale_vector,
    headwise_additive_matrix,
    product_scale_vector,
    first_factor_matrix,
    other_factor_matrix,
    product_mapping_matrix,
):
    g2 = product_scale_vector.reshape(1, 256)
    flags = position_valid_flags.reshape(2, 128)
    first, other = first_factor_matrix.T, other_factor_matrix.T

    message, gate, prior, right = pl.pallas_call(
        front_kernel,
        grid=(2,),
        in_specs=[SCALARS, pl.BlockSpec((16, 256, 128), lambda i: (i, 0, 0))]
        + [
            whole(s)
            for s in (
                (512, 256),
                (2, 128),
                (1, 256),
                (256, 256),
                (256, 256),
                (256, 256),
                (256, 256),
                (1, 128),
                (8, 128),
                (1, 256),
                (32, 256),
            )
        ],
        out_specs=[whole((8, 176, 256)), whole((64, 256)), whole((64, 256)), whole((2, 32, 256))],
        out_shape=[
            jax.ShapeDtypeStruct((8, 176, 256), BF16),
            jax.ShapeDtypeStruct((64, 256), F32),
            jax.ShapeDtypeStruct((64, 256), F32),
            jax.ShapeDtypeStruct((2, 32, 256), BF16),
        ],
        scratch_shapes=[pltpu.VMEM((2, 256, 128), F32), pltpu.VMEM((4, 512, 128), F32)],
        compiler_params=pltpu.CompilerParams(vmem_limit_bytes=FULL),
    )(
        sequence_valid_flags,
        couple_activity,
        sequence_activity.reshape(512, 256),
        flags,
        attend_scale_vector.reshape(1, 256),
        asking_matrix,
        lookup_matrix,
        content_matrix,
        sigmoid_matrix,
        couple_scale_vector.reshape(1, 128),
        headwise_additive_matrix.T,
        g2,
        other,
    )

    heads = lax.all_to_all(message, "q", 0, 0, tiled=True)
    x0 = lax.ppermute(right, ALL, MIRROR)
    mapping = pl.pallas_call(
        line_kernel,
        in_specs=[ARRAY],
        out_specs=ARRAY,
        out_shape=jax.ShapeDtypeStruct((128, 4096), BF16),
        scratch_shapes=[pltpu.VMEM((1024, 128), F32)],
        compiler_params=params(),
    )(product_mapping_matrix)
    heads, x0, mapping = lax.optimization_barrier((heads, x0, mapping))
    kv = heads[:, 32:176, :]
    own = heads[:, 160:176, 0:128]
    kva = lax.ppermute(kv, ("c", "x"), ACROSS)
    kvb = lax.ppermute(kv, ("c", "x"), ACROSS_NEXT)
    swapped = lax.ppermute(own, "x", SWAP)
    x1 = lax.ppermute(x0, "x", SWAP)
    below, above = [heads[:, 0:32, :]], [heads[:, 0:32, :]]
    for step in range(4):
        below.append(lax.ppermute(below[-1], ("c", "z"), AHEAD))
        if step < 3:
            above.append(lax.ppermute(above[-1], ("c", "z"), BEHIND))
        if step == 2:
            below[3], swapped = lax.optimization_barrier((below[3], swapped))


    state = pl.pallas_call(
        attend_kernel,
        in_specs=[ARRAY] * 11,
        out_specs=ARRAY,
        out_shape=jax.ShapeDtypeStruct((2, 3, 128, 128), F32),
        scratch_shapes=[pltpu.VMEM((2, 128, 7 * 256), F32)],
        compiler_params=params(),
    )(own, swapped, kva, kvb, below[0], below[1], above[1], below[2], above[2], below[3], above[3])
    parts = pl.pallas_call(
        finish_kernel,
        in_specs=[ARRAY] * 8,
        out_specs=ARRAY,
        out_shape=jax.ShapeDtypeStruct((8, 2, 48, 256), BF16),
        scratch_shapes=[pltpu.VMEM((2, 128, 256), F32)],
        compiler_params=params(),
    )(own, swapped, kva, kvb, below[4], state, x0, x1)

    parts = lax.all_to_all(parts.reshape(16, 48, 256), ("q", "x"), 0, 0, tiled=True)

    fresh, sides = pl.pallas_call(
        refresh_kernel,
        in_specs=[SCALARS] + [ARRAY] * 8,
        out_specs=[ARRAY] * 2,
        out_shape=[jax.ShapeDtypeStruct((64, 256), BF16), jax.ShapeDtypeStruct((32, 128), BF16)],
        compiler_params=params(),
    )(sequence_valid_flags, parts, gate, prior, flags, attend_final_matrix, g2, first, other)

    sides = gather(sides, ("z", "x"), 16)
    band = lax.ppermute(sides[:, 16:32, :], ALL, MIRROR)
    parts, sides = lax.optimization_barrier((parts, sides))
    theirs = lax.ppermute(parts[:, 16:48, :], "c", SWAP)
    factors = pl.pallas_call(
        pack_kernel,
        in_specs=[ARRAY] * 2,
        out_specs=ARRAY,
        out_shape=jax.ShapeDtypeStruct((256, 1024), BF16),
        scratch_shapes=[pltpu.VMEM((2, 1024, 128), F32)],
        cost_estimate=pl.CostEstimate(flops=0, bytes_accessed=4 << 20, transcendentals=0),
        compiler_params=params(),
    )(parts, theirs)
    mapped = pl.pallas_call(
        map_kernel,
        grid=(4,),
        in_specs=[whole((16, 32, 128)), whole((128, 4096))],
        out_specs=pl.BlockSpec((4, 1024, 256), lambda i: (i, 0, 0)),
        out_shape=jax.ShapeDtypeStruct((16, 1024, 256), BF16),
        scratch_shapes=[pltpu.VMEM((256, 128), F32)],
        cost_estimate=pl.CostEstimate(flops=4 << 30, bytes_accessed=20 << 20, transcendentals=0),
        compiler_params=params(),
    )(sides, mapping)
    pair_out = pl.pallas_call(
        outer_kernel,
        in_specs=[SCALARS] * 2 + [ARRAY] * 4,
        out_specs=pl.BlockSpec(memory_space=pl.ANY),
        out_shape=jax.ShapeDtypeStruct((32, 256, 128), BF16),
        scratch_shapes=[
            pltpu.VMEM((1024, 128), F32),
            pltpu.VMEM((256, 1024), BF16),
            pltpu.VMEM((32, 256, 128), BF16),
            pltpu.SemaphoreType.DMA((8,)),
        ],
        compiler_params=params(),
    )(sequence_valid_flags, position_valid_flags, factors, band, mapped, couple_activity)
    return fresh.reshape(2, 32, 256), pair_out


def solution(mesh):
    mesh = Mesh(mesh.devices.reshape(8, 2, 8, 2), ALL)
    wide, narrow = ("q", "c"), ("z", "x")
    in_specs = (P(narrow, wide, None), P(wide, narrow, None), P(), P(wide)) + (P(),) * 12
    out_specs = (P(narrow, wide, None), P(wide, narrow, None))
    return jax.shard_map(local, mesh=mesh, in_specs=in_specs, out_specs=out_specs, check_vma=False)
```

```python
import jax
import jax.numpy as jnp
from jax import lax
from jax.experimental import pallas as pl
from jax.experimental.pallas import tpu as pltpu
from jax.sharding import Mesh, PartitionSpec as P

EPS = 1e-05
BIG = 1000000000.0
F32 = jnp.float32
BF16 = jnp.bfloat16
VMEM = 40 * 1024 * 1024
FULL = 60 * 1024 * 1024
ALL = ("q", "c", "z", "x")


def dot(a, b, dims):
    return lax.dot_general(a, b, (dims, ((), ())), preferred_element_type=F32)


NN = ((1,), (0,))
NT = ((1,), (1,))
TN = ((0,), (0,))
TT = ((0,), (1,))


def center_and_scale(values):
    center = values - jnp.mean(values, axis=-1, keepdims=True)
    spread = jnp.mean(center * center, axis=-1, keepdims=True)
    return center * lax.rsqrt(spread + EPS)


def row_of(flags, count):
    lane = lax.broadcasted_iota(jnp.int32, (count, 256), 1)
    row = lax.broadcasted_iota(jnp.int32, (count, 256), 0)
    return jnp.sum(jnp.where(lane == row * 8, flags, 0.0), axis=1, keepdims=True)


def front_kernel(
    live_ref,
    pair_ref,
    seq_ref,
    flags_ref,
    g1_ref,
    ask_ref,
    look_ref,
    cont_ref,
    gp_ref,
    head_ref,
    g2_ref,
    other_ref,
    msg_ref,
    right_ref,
    bias_scr,
    norm_scr,
):
    step = pl.program_id(0)
    rows = pair_ref.shape[0]
    first_row = (lax.axis_index("z") * 2 + lax.axis_index("x")) * 2

    pair = pair_ref[...].reshape(rows * 256, 128).astype(F32)
    pair = (center_and_scale(pair) * gp_ref[...]).astype(BF16)
    bias = dot(head_ref[...], pair, NT)
    for r in range(rows):
        for i in range(2):
            bias_scr[i, pl.ds(pl.multiple_of((step * rows + r) * 8, 8), 8), :] = bias[
                :, r * 256 + i * 128 : r * 256 + i * 128 + 128
            ]

    @pl.when(step == 0)
    def _():
        base = center_and_scale(seq_ref[...].astype(F32))
        normed = (base * g1_ref[...]).astype(BF16)
        keys = dot(look_ref[...], normed, TT).astype(BF16)
        values = dot(cont_ref[...], normed, TT).astype(BF16)
        for h in range(8):
            for s in range(2):
                cut = (slice(h * 32, h * 32 + 32), slice(s * 256, s * 256 + 256))
                msg_ref[h, 32 + s * 32 : 64 + s * 32, :] = keys[cut]
                msg_ref[h, 96 + s * 32 : 128 + s * 32, :] = values[cut]
        wide = normed.astype(F32)
        for i in range(2):
            norm_scr[i] = wide[:, i * 128 : (i + 1) * 128]
        band = jnp.concatenate(
            [norm_scr[i, pl.ds(0, 64, stride=8), :] for i in range(2)], axis=1
        ).astype(BF16)
        query = (dot(band, ask_ref[...], NN) * 32 ** (-0.5)).astype(BF16).astype(F32)
        flags = flags_ref[...].astype(F32)
        row = lax.broadcasted_iota(jnp.int32, (16, 128), 0)
        mask = jnp.where(row == 0, flags[0:1], jnp.where(row == 1, flags[1:2], 0.0))
        for h in range(8):
            parts = [
                query[s * 32 + g * 16 : s * 32 + g * 16 + 16, h * 32 : h * 32 + 32]
                for g in range(2)
                for s in range(2)
            ]
            msg_ref[h, 160:176, :] = jnp.concatenate(parts + [mask], axis=1).astype(BF16)
        again = (base * g2_ref[...]).astype(BF16)
        right = dot(other_ref[...], again, NT)
        flags = jnp.concatenate([flags[0:1], flags[1:2]], axis=1)
        for s in range(2):
            live = live_ref[first_row + s].astype(F32) * flags
            right_ref[s] = (right[:, s * 256 : (s + 1) * 256] * live).astype(BF16)

    @pl.when(step == pl.num_programs(0) - 1)
    def _():
        for h in range(8):
            for i in range(2):
                msg_ref[h, 0:32, i * 128 : i * 128 + 128] = bias_scr[
                    i, pl.ds(h, 32, stride=8), :
                ].astype(BF16)


def split3(value):
    high = value.astype(BF16).astype(F32)
    rest = value - high
    middle = rest.astype(BF16).astype(F32)
    return high, middle, rest - middle


def attend_blocks(own_ref, swapped_ref, kva_ref, kvb_ref, blocks, extra_scr):
    c, x, z = lax.axis_index("c"), lax.axis_index("x"), lax.axis_index("z")
    places = [lax.rem(z + offset * (1 - 2 * c) + 8, 8) for offset, _ in blocks]
    block = lax.broadcasted_iota(jnp.int32, (128, 128), 1) // 32
    for k, (place, (_, bias_ref)) in enumerate(zip(places, blocks)):
        tile = kva_ref[place, 128:144, 128:256].astype(F32)
        mask = jnp.concatenate([tile[0:1], tile[1:2]], axis=1)
        for g in range(2):
            piece = bias_ref[:, g * 16 : g * 16 + 16, :].reshape(128, 256).astype(F32)
            extra_scr[g, :, k * 256 : (k + 1) * 256] = piece + BIG * (mask - 1.0)
    own = own_ref[...].reshape(128, 128)
    swapped = swapped_ref[...].reshape(128, 128)
    states = []
    for a, kv_ref in enumerate((kva_ref, kvb_ref)):
        query = jnp.where((c ^ a) == x, own, swapped).astype(F32)
        keys = jnp.concatenate([kv_ref[place, 0:64, :] for place in places], axis=1)
        values = jnp.concatenate([kv_ref[place, 64:128, :] for place in places], axis=1)
        keys = jnp.concatenate([keys, keys], axis=0)
        values = jnp.concatenate([values, values], axis=0)
        state = [jnp.zeros((128, 128), F32)] * 3
        for g in range(2):
            for s in range(2):
                here = block == g * 2 + s
                picked = jnp.where(here, query, 0.0).astype(BF16)
                scores = dot(picked, keys, NN) + extra_scr[g]
                top = jnp.max(scores, axis=1, keepdims=True)
                expo = jnp.exp(scores - top)
                total = jnp.sum(expo, axis=1, keepdims=True)
                mixed = dot(expo.astype(BF16), values, NT)
                state = [jnp.where(here, new, old) for new, old in zip((mixed, top, total), state)]
        states.append(state)
    return states


def attend_kernel(own_ref, swapped_ref, kva_ref, kvb_ref, *refs):
    *bias_refs, out_ref, extra_scr = refs
    blocks = list(zip((0, -1, 1, -2, 2, -3, 3), bias_refs))
    states = attend_blocks(own_ref, swapped_ref, kva_ref, kvb_ref, blocks, extra_scr)
    for a in range(2):
        for i in range(3):
            out_ref[a, i] = states[a][i]


def finish_kernel(own_ref, swapped_ref, kva_ref, kvb_ref, *refs):
    *bias_refs, state_ref, x0_ref, x1_ref, out_ref, extra_scr = refs
    c, x = lax.axis_index("c"), lax.axis_index("x")
    for q in range(8):
        out_ref[q, x, 16:48, :] = x0_ref[x]
        out_ref[q, 1 - x, 16:48, :] = x1_ref[x]
    inner = lax.broadcasted_iota(jnp.int32, (128, 128), 1) % 32
    blocks = list(zip((-4,), bias_refs))
    states = attend_blocks(own_ref, swapped_ref, kva_ref, kvb_ref, blocks, extra_scr)
    for a in range(2):
        mixed, top, total = states[a]
        other_mixed, other_top, other_total = (state_ref[a, i] for i in range(3))
        best = jnp.maximum(top, other_top)
        weight, other_weight = jnp.exp(top - best), jnp.exp(other_top - best)
        total = total * weight + other_total * other_weight
        mixed = (mixed * weight + other_mixed * other_weight) / total
        stats = jnp.zeros((128, 128), F32)
        for t, piece in enumerate(split3(best) + split3(total)):
            stats = jnp.where(inner == t, piece, stats)
        joined = jnp.concatenate([mixed, stats], axis=1).astype(BF16)
        for q in range(8):
            out_ref[q, c ^ a, 0:16, :] = joined[q * 16 : q * 16 + 16]


def refresh_kernel(
    parts_ref,
    gate_ref,
    prior_ref,
    alive_ref,
    final_ref,
    g2_ref,
    first_ref,
    other_ref,
    fresh_ref,
    sides_ref,
):
    rows = lax.broadcasted_iota(jnp.int32, (128, 128), 0)
    lanes = lax.broadcasted_iota(jnp.int32, (128, 128), 1)
    spread = jnp.concatenate(
        [jnp.where(rows == (lanes // 32) * 32 + t, 1.0, 0.0).astype(BF16) for t in range(6)], axis=1
    )
    tops, totals, mixes = [], [], []
    for x in range(2):
        mixes.append(
            jnp.concatenate([parts_ref[2 * h + x, 0:16, 0:128] for h in range(8)], axis=0).astype(F32)
        )
        stats = jnp.concatenate([parts_ref[2 * h + x, 0:16, 128:256] for h in range(8)], axis=0)
        wide = dot(stats, spread, NN)
        wide = [wide[:, t * 128 : (t + 1) * 128] for t in range(6)]
        tops.append(wide[0] + wide[1] + wide[2])
        totals.append(wide[3] + wide[4] + wide[5])
    top = jnp.maximum(tops[0], tops[1])
    weights = [totals[i] * jnp.exp(tops[i] - top) for i in range(2)]
    attended = (weights[0] * mixes[0] + weights[1] * mixes[1]) / (weights[0] + weights[1])
    lined = []
    for s in range(2):
        for g in range(2):
            cut = (g * 2 + s) * 32
            lined.append(
                jnp.concatenate(
                    [attended[h * 16 : h * 16 + 16, cut : cut + 32] for h in range(8)], axis=1
                )
            )
    attended = jnp.concatenate(lined, axis=0)
    gated = (gate_ref[...] * attended).astype(BF16)
    fresh = (prior_ref[...] + dot(gated, final_ref[...], NN)).astype(BF16)
    fresh_ref[...] = fresh
    again = (center_and_scale(fresh.astype(F32)) * g2_ref[...]).astype(BF16)
    for i, factor in enumerate((first_ref, other_ref)):
        side = dot(again, factor[...], NT) * alive_ref[...]
        parts = [side[s * 32 + g * 16 : s * 32 + g * 16 + 16] for g in range(2) for s in range(2)]
        sides_ref[i * 16 : i * 16 + 16, :] = jnp.concatenate(parts, axis=1).astype(BF16)


def pack_kernel(mine_ref, theirs_ref, factors_ref, factor_scr):
    swapped = lax.axis_index("c") == 1
    turn = lax.axis_index("z") * 2 + lax.axis_index("x")
    for q in range(8):
        for c in range(2):
            for x in range(2):
                mine = mine_ref[2 * q + x, 16:48, :].astype(F32)
                theirs = theirs_ref[2 * q + x].astype(F32)
                piece = jnp.where(swapped == (c == 1), mine, theirs)
                place = pl.multiple_of((x * 16 + (turn ^ (2 * q + c))) * 32, 32)
                for i in range(2):
                    factor_scr[i, pl.ds(place, 32), :] = piece[:, i * 128 : i * 128 + 128]
    for k in range(8):
        rows = []
        for d in range(k * 4, k * 4 + 4):
            rows.append(
                jnp.concatenate([factor_scr[i, pl.ds(d, 32, stride=32), :] for i in range(2)], axis=1)
            )
        factors_ref[:, k * 128 : (k + 1) * 128] = jnp.concatenate(rows, axis=0).T.astype(BF16)


def side_kernel(
    live_ref, seq_ref, flags_ref, g1_ref, sig_ref, map_ref, gate_ref, prior_ref, alive_ref, mapping_ref, seq_scr, scr
):
    for i in range(2):
        seq_scr[i] = seq_ref[:, i * 128 : (i + 1) * 128].astype(F32)
    prior = jnp.concatenate([seq_scr[i, pl.ds(0, 64, stride=8), :] for i in range(2)], axis=1)
    prior_ref[...] = prior
    band = (center_and_scale(prior) * g1_ref[...]).astype(BF16)
    gate_ref[...] = jax.nn.sigmoid(dot(band, sig_ref[...], NN))
    first_row = (lax.axis_index("z") * 2 + lax.axis_index("x")) * 2
    flags = flags_ref[...].astype(F32)
    column = row_of(jnp.concatenate([flags[0:1], flags[1:2]], axis=1), 32)
    live = jnp.concatenate([column * live_ref[first_row + s].astype(F32) for s in range(2)], axis=0)
    alive_ref[...] = jnp.broadcast_to(live, (64, 32))
    scr[...] = map_ref[...].astype(F32)
    for d in range(32):
        piece = scr[pl.ds(d, 32, stride=32), :].astype(BF16)
        for k in range(4):
            mapping_ref[k * 32 : k * 32 + 32, d * 128 : (d + 1) * 128] = piece


def map_kernel(sides_ref, mapping_ref, out_ref, side_scr):
    step = pl.program_id(0)

    @pl.when(step == 0)
    def _():
        for n in range(16):
            side_scr[n * 16 : n * 16 + 16, :] = sides_ref[n, 0:16, :].astype(F32)

    block = lax.broadcasted_iota(jnp.int32, (16, 128), 1) // 32
    group = step // 2
    lefts = []
    for r in range(8):
        lined = side_scr[pl.ds((step % 2) * 8 + r, 16, stride=16), :]
        for s in range(2):
            lefts.append(jnp.where(block == group * 2 + s, lined, 0.0))
    left = jnp.concatenate(lefts, axis=0).astype(BF16)
    for d in range(0, 32, 2):
        mapped = dot(left, mapping_ref[:, d * 128 : (d + 2) * 128], NN).astype(BF16)
        for e in range(2):
            for r in range(8):
                out_ref[r // 2, (d + e) * 32 : (d + e) * 32 + 32, (r % 2) * 128 : (r % 2) * 128 + 128] = (
                    mapped[r * 32 : r * 32 + 32, e * 128 : e * 128 + 128]
                )


def outer_kernel(
    live_ref,
    flags_ref,
    factors_ref,
    band_ref,
    mapped_ref,
    pair_ref,
    out_ref,
    band_scr,
    full_scr,
    done_scr,
    sems,
):
    turned = jnp.concatenate([band_ref[n].astype(F32) for n in range(16)], axis=0).T
    empty = jnp.zeros((32, 96), F32)
    for s in range(2):
        for n in range(16):
            parts = [
                turned[g * 64 + s * 32 : g * 64 + s * 32 + 32, n * 16 : n * 16 + 16] for g in range(2)
            ]
            band_scr[pl.ds(s * 16 + n, 32, stride=32), :] = jnp.concatenate(parts + [empty], axis=1)
    slot = lax.broadcasted_iota(jnp.int32, (256, 128), 0) % 8
    for i in range(8):
        band = band_scr[i * 128 : (i + 1) * 128, :].T[0:32]
        band = jnp.broadcast_to(band[:, None, :], (32, 8, 128)).reshape(256, 128)
        piece = factors_ref[:, i * 128 : (i + 1) * 128].astype(F32)
        full_scr[:, i * 128 : (i + 1) * 128] = jnp.where(slot == 0, band, piece).astype(BF16)

    nvalid = jnp.int32(0)
    for s in range(32):
        nvalid += live_ref[s]
    copies = []
    for k in range(8):
        for r in range(k * 4, k * 4 + 4, 2):
            projected = dot(full_scr[...], mapped_ref[r // 2], NN)
            for i in range(2):
                scale = 1.0 / jnp.maximum((nvalid * flags_ref[(r + i) * 8]).astype(F32), 1.0)
                done_scr[r + i] = (
                    pair_ref[r + i].astype(F32) + projected[:, i * 128 : (i + 1) * 128] * scale
                ).astype(BF16)
        part = pl.ds(k * 4, 4)
        copies.append(pltpu.make_async_copy(done_scr.at[part], out_ref.at[part], sems.at[k]))
        copies[-1].start()
    for copy in copies:
        copy.wait()


def gather(value, axes, count):
    tiled = jnp.broadcast_to(value[None], (count,) + value.shape)
    return lax.all_to_all(tiled, axes, 0, 0, tiled=True)


def whole(shape):
    return pl.BlockSpec(shape, lambda *_: (0,) * len(shape))


SCALARS = pl.BlockSpec(memory_space=pltpu.SMEM)
ARRAY = pl.BlockSpec(memory_space=pltpu.VMEM)


def params():
    return pltpu.CompilerParams(vmem_limit_bytes=VMEM)


MIRROR = [(w * 16 + n, (n ^ w) * 16 + w) for w in range(16) for n in range(16)]
ACROSS = [(a * 2 + b, b * 2 + a) for a in range(2) for b in range(2)]
ACROSS_NEXT = [(a * 2 + b, (1 - b) * 2 + a) for a in range(2) for b in range(2)]
SWAP = [(0, 1), (1, 0)]
AHEAD = [(c * 8 + i, c * 8 + (i + 1 - 2 * c) % 8) for c in range(2) for i in range(8)]
BEHIND = [(c * 8 + i, c * 8 + (i - 1 + 2 * c) % 8) for c in range(2) for i in range(8)]


def local(
    sequence_activity,
    couple_activity,
    sequence_valid_flags,
    position_valid_flags,
    attend_scale_vector,
    asking_matrix,
    lookup_matrix,
    content_matrix,
    sigmoid_matrix,
    attend_final_matrix,
    couple_scale_vector,
    headwise_additive_matrix,
    product_scale_vector,
    first_factor_matrix,
    other_factor_matrix,
    product_mapping_matrix,
):
    g2 = product_scale_vector.reshape(1, 256)
    flags = position_valid_flags.reshape(2, 128)
    first, other = first_factor_matrix.T, other_factor_matrix.T

    seq = sequence_activity.reshape(512, 256)
    g1 = attend_scale_vector.reshape(1, 256)
    message, right = pl.pallas_call(
        front_kernel,
        grid=(2,),
        in_specs=[SCALARS, pl.BlockSpec((16, 256, 128), lambda i: (i, 0, 0))]
        + [
            whole(s)
            for s in (
                (512, 256),
                (2, 128),
                (1, 256),
                (256, 256),
                (256, 256),
                (256, 256),
                (1, 128),
                (8, 128),
                (1, 256),
                (32, 256),
            )
        ],
        out_specs=[whole((8, 176, 256)), whole((2, 32, 256))],
        out_shape=[
            jax.ShapeDtypeStruct((8, 176, 256), BF16),
            jax.ShapeDtypeStruct((2, 32, 256), BF16),
        ],
        scratch_shapes=[pltpu.VMEM((2, 256, 128), F32), pltpu.VMEM((2, 512, 128), F32)],
        compiler_params=pltpu.CompilerParams(vmem_limit_bytes=FULL),
    )(
        sequence_valid_flags,
        couple_activity,
        seq,
        flags,
        g1,
        asking_matrix,
        lookup_matrix,
        content_matrix,
        couple_scale_vector.reshape(1, 128),
        headwise_additive_matrix.T,
        g2,
        other,
    )

    heads = lax.all_to_all(message, "q", 0, 0, tiled=True)
    x0 = lax.ppermute(right, ALL, MIRROR)
    gate, prior, alive, mapping = pl.pallas_call(
        side_kernel,
        in_specs=[SCALARS] + [ARRAY] * 5,
        out_specs=[ARRAY] * 4,
        out_shape=[
            jax.ShapeDtypeStruct((64, 256), F32),
            jax.ShapeDtypeStruct((64, 256), F32),
            jax.ShapeDtypeStruct((64, 32), F32),
            jax.ShapeDtypeStruct((128, 4096), BF16),
        ],
        scratch_shapes=[pltpu.VMEM((2, 512, 128), F32), pltpu.VMEM((1024, 128), F32)],
        compiler_params=params(),
    )(sequence_valid_flags, seq, flags, g1, sigmoid_matrix, product_mapping_matrix)
    heads, x0, mapping = lax.optimization_barrier((heads, x0, mapping))
    kv = heads[:, 32:176, :]
    own = heads[:, 160:176, 0:128]
    kva = lax.ppermute(kv, ("c", "x"), ACROSS)
    kvb = lax.ppermute(kv, ("c", "x"), ACROSS_NEXT)
    swapped = lax.ppermute(own, "x", SWAP)
    x1 = lax.ppermute(x0, "x", SWAP)
    below, above = [heads[:, 0:32, :]], [heads[:, 0:32, :]]
    for step in range(4):
        below.append(lax.ppermute(below[-1], ("c", "z"), AHEAD))
        if step < 3:
            above.append(lax.ppermute(above[-1], ("c", "z"), BEHIND))
        if step == 2:
            below[3], swapped = lax.optimization_barrier((below[3], swapped))


    state = pl.pallas_call(
        attend_kernel,
        in_specs=[ARRAY] * 11,
        out_specs=ARRAY,
        out_shape=jax.ShapeDtypeStruct((2, 3, 128, 128), F32),
        scratch_shapes=[pltpu.VMEM((2, 128, 7 * 256), F32)],
        compiler_params=params(),
    )(own, swapped, kva, kvb, below[0], below[1], above[1], below[2], above[2], below[3], above[3])
    parts = pl.pallas_call(
        finish_kernel,
        in_specs=[ARRAY] * 8,
        out_specs=ARRAY,
        out_shape=jax.ShapeDtypeStruct((8, 2, 48, 256), BF16),
        scratch_shapes=[pltpu.VMEM((2, 128, 256), F32)],
        compiler_params=params(),
    )(own, swapped, kva, kvb, below[4], state, x0, x1)

    parts = lax.all_to_all(parts.reshape(16, 48, 256), ("q", "x"), 0, 0, tiled=True)

    fresh, sides = pl.pallas_call(
        refresh_kernel,
        in_specs=[ARRAY] * 8,
        out_specs=[ARRAY] * 2,
        out_shape=[jax.ShapeDtypeStruct((64, 256), BF16), jax.ShapeDtypeStruct((32, 128), BF16)],
        compiler_params=params(),
    )(parts, gate, prior, alive, attend_final_matrix, g2, first, other)

    sides = gather(sides, ("z", "x"), 16)
    band = lax.ppermute(sides[:, 16:32, :], ALL, MIRROR)
    parts, sides = lax.optimization_barrier((parts, sides))
    theirs = lax.ppermute(parts[:, 16:48, :], "c", SWAP)
    factors = pl.pallas_call(
        pack_kernel,
        in_specs=[ARRAY] * 2,
        out_specs=ARRAY,
        out_shape=jax.ShapeDtypeStruct((256, 1024), BF16),
        scratch_shapes=[pltpu.VMEM((2, 1024, 128), F32)],
        cost_estimate=pl.CostEstimate(flops=0, bytes_accessed=4 << 20, transcendentals=0),
        compiler_params=params(),
    )(parts, theirs)
    mapped = pl.pallas_call(
        map_kernel,
        grid=(4,),
        in_specs=[whole((16, 32, 128)), whole((128, 4096))],
        out_specs=pl.BlockSpec((4, 1024, 256), lambda i: (i, 0, 0)),
        out_shape=jax.ShapeDtypeStruct((16, 1024, 256), BF16),
        scratch_shapes=[pltpu.VMEM((256, 128), F32)],
        cost_estimate=pl.CostEstimate(flops=4 << 30, bytes_accessed=20 << 20, transcendentals=0),
        compiler_params=params(),
    )(sides, mapping)
    pair_out = pl.pallas_call(
        outer_kernel,
        in_specs=[SCALARS] * 2 + [ARRAY] * 4,
        out_specs=pl.BlockSpec(memory_space=pl.ANY),
        out_shape=jax.ShapeDtypeStruct((32, 256, 128), BF16),
        scratch_shapes=[
            pltpu.VMEM((1024, 128), F32),
            pltpu.VMEM((256, 1024), BF16),
            pltpu.VMEM((32, 256, 128), BF16),
            pltpu.SemaphoreType.DMA((8,)),
        ],
        compiler_params=params(),
    )(sequence_valid_flags, position_valid_flags, factors, band, mapped, couple_activity)
    return fresh.reshape(2, 32, 256), pair_out


def solution(mesh):
    mesh = Mesh(mesh.devices.reshape(8, 2, 8, 2), ALL)
    wide, narrow = ("q", "c"), ("z", "x")
    in_specs = (P(narrow, wide, None), P(wide, narrow, None), P(), P(wide)) + (P(),) * 12
    out_specs = (P(narrow, wide, None), P(wide, narrow, None))
    return jax.shard_map(local, mesh=mesh, in_specs=in_specs, out_specs=out_specs, check_vma=False)
```
